32 devices in a mesh: seq: 32 (over z, y, x, core), tp: 1.
Axes of the slice: x: 2, y: 2, z: 4, core: 2. Of those that a mesh axis runs over, the one named last changes fastest.
Arguments:
- queries: bfloat16 [4096, 2048], P('seq', 'tp'), may hold values from -4.5 to 4.5
- keys: bfloat16 [4096, 2048], P('seq', 'tp'), may hold values from -4.5 to 4.5
- values: bfloat16 [4096, 2048], P('seq', 'tp'), may hold values from -6 to 6
- step_rate: float32 [16], P('tp'), may hold values from 0.0078125 to 0.25
- memory_init: float32 [16, 128, 128], P('tp'), may hold values from -0.5 to 0.5
- out_weight: bfloat16 [2048, 2048], P('tp'), may hold values from -0.125 to 0.125
Outputs:
- layer_out: bfloat16 [4096, 2048], P('seq', 'tp')
The draws below stay inside these ranges and needn't reach their ends.
All inputs are finite; a program needn't handle non-finite values.
Results may differ from the reference program's by a relative error of at most 0.018.
Values may be sent and summed in bfloat16 or wider, within the bound.
No kernel may reach another device: no remote copies, remote signals or barrier semaphores. Data moves between devices by JAX's collectives and lax.ppermute only.
A program may use at most 192 MiB of HBM per device.

```python
import math
import jax
import jax.numpy as jnp
from jax import lax

H = 16
HD = 128
D = 2048
WIN = 1024
CH = 16
TOKENS = 4096


def paired_rows(key):
    width = H * HD
    queries_out = jnp.clip(jax.random.normal(jax.random.fold_in(key, 201), (TOKENS, width), jnp.float32), -4.5, 4.5)
    keys_out = jnp.clip(jax.random.normal(jax.random.fold_in(key, 202), (TOKENS, width), jnp.float32), -4.5, 4.5)
    return (queries_out, keys_out)


def draw_queries(key, part):
    return paired_rows(key)[0].astype(jnp.bfloat16)


def draw_keys(key, part):
    return paired_rows(key)[1].astype(jnp.bfloat16)


def level_of(rng, extent, split, low, high):
    level = 1.0
    for axis_at, shards_of in split:
        heights = jax.random.uniform(jax.random.fold_in(jax.random.fold_in(rng, 6), axis_at), (shards_of,), jnp.float32, low / len(split), high / len(split))
        level = level * jnp.repeat(jnp.exp(heights), extent[axis_at] // shards_of).reshape((-1,) + (1,) * (len(extent) - 1 - axis_at))
    return level


def centred(stream_key, shape, scale, reach, shards=(), kind=jnp.bfloat16):
    values = jax.random.normal(stream_key, shape, jnp.float32) * scale
    if len(shards) > 0:
        values = level_of(stream_key, shape, shards, -0.22, 0.18) * values
    return jnp.clip(values, min=-reach, max=reach).astype(kind)


def setup_inputs(seed: int = 0) -> dict:
    streams_of = jax.random.split(jax.random.key(seed), 7)
    queries = draw_queries(jax.random.fold_in(streams_of[6], 71), 0)
    keys = draw_keys(jax.random.fold_in(streams_of[6], 71), 0)
    values = centred(streams_of[2], (TOKENS, H * HD), 1.0, 6.0, ((0, 32),))
    step_rate = jnp.clip(jnp.exp(jax.random.uniform(streams_of[3], (H,), jnp.float32, math.log(0.0078125), math.log(0.25))), 0.0078125, 0.25)
    memory_init = centred(streams_of[4], (H, HD, HD), HD ** -0.5, 0.5, (), jnp.float32)
    out_weight = centred(streams_of[5], (H * HD, D), (H * HD) ** -0.5, 0.125)
    return {"queries": queries, "keys": keys, "values": values, "step_rate": step_rate, "memory_init": memory_init, "out_weight": out_weight}


highest = lax.Precision.HIGHEST

def unit_keys(keys_float):
    mean_square = lax.optimization_barrier(jnp.mean(keys_float * keys_float, axis=-1, keepdims=True))
    return keys_float / jnp.sqrt(HD * (mean_square + 1e-06))

def reference(queries, keys, values, step_rate, memory_init, out_weight):
    q_heads = queries.reshape(TOKENS, H, HD)
    k_heads = keys.reshape(TOKENS, H, HD)
    v_heads = values.reshape(TOKENS, H, HD)
    group_count = TOKENS // CH
    query_blocks = q_heads.astype(jnp.float32).reshape(group_count, CH, H, HD)
    key_blocks = unit_keys(k_heads.astype(jnp.float32)).reshape(group_count, CH, H, HD)
    value_blocks = v_heads.astype(jnp.float32).reshape(group_count, CH, H, HD)

    def update(memory, blocks):
        query_blk, key_blk, value_blk = blocks
        readout = jnp.einsum('thi,hij->thj', query_blk, memory, precision=highest)
        errors = jnp.einsum('thi,hij->thj', key_blk, memory, precision=highest) - value_blk
        gradient = jnp.einsum('thi,thj->hij', key_blk, errors, precision=highest)
        return (memory - step_rate[:, None, None] * gradient, readout)
    final_memory, readouts = lax.scan(update, memory_init.astype(jnp.float32), (query_blocks, key_blocks, value_blocks))
    memory_read = readouts.reshape(TOKENS, H, HD)
    query_block = math.gcd(512, TOKENS)
    block_count = TOKENS // query_block
    span_len = WIN + query_block
    key_padded = jnp.concatenate([jnp.zeros((WIN, H, HD), k_heads.dtype), k_heads], axis=0)
    value_padded = jnp.concatenate([jnp.zeros((WIN, H, HD), v_heads.dtype), v_heads], axis=0)

    def attend(block_index):
        offset = (block_index * query_block).astype(jnp.int32)
        query_part = lax.dynamic_slice_in_dim(q_heads, offset, query_block, 0).astype(jnp.float32)
        key_part = lax.dynamic_slice_in_dim(key_padded, offset, span_len, 0).astype(jnp.float32)
        value_part = lax.dynamic_slice_in_dim(value_padded, offset, span_len, 0).astype(jnp.float32)
        query_pos = offset + jnp.arange(query_block, dtype=jnp.int32)
        key_pos = offset - WIN + jnp.arange(span_len, dtype=jnp.int32)
        allowed = (key_pos[None, :] <= query_pos[:, None]) & (key_pos[None, :] > query_pos[:, None] - WIN) & (key_pos[None, :] >= 0)
        scores = jnp.einsum('qhd,khd->hqk', query_part, key_part) * (1.0 / math.sqrt(HD))
        scores = jnp.where(allowed[None], scores, -jnp.inf)
        maxima = lax.optimization_barrier(jnp.max(scores, axis=-1, keepdims=True))
        expd = jnp.where(allowed[None], jnp.exp(scores - maxima), 0.0)
        totals = lax.optimization_barrier(jnp.sum(expd, axis=-1, keepdims=True))
        probs = (expd / totals).astype(jnp.bfloat16)
        return jnp.einsum('hqk,khd->qhd', probs.astype(jnp.float32), value_part)
    attended = lax.map(attend, jnp.arange(block_count, dtype=jnp.int32)).reshape(TOKENS, H, HD)
    gated = (attended * jax.nn.sigmoid(memory_read)).astype(jnp.bfloat16).reshape(TOKENS, H * HD)
    return jnp.dot(gated, out_weight, preferred_element_type=jnp.float32).astype(jnp.bfloat16)
```

```python
import functools
import math

import jax
import jax.numpy as jnp
from jax import lax
from jax.experimental import pallas as pl
from jax.experimental.pallas import tpu as pltpu
from jax.sharding import PartitionSpec as P

WIN = 1024
CH = 16
BLK = 128
MASKED = -1e30
F32 = jnp.float32
BF16 = jnp.bfloat16


def dot(a, b):
    return jnp.dot(a.astype(BF16), b.astype(BF16), preferred_element_type=F32)


def dot_nt(a, b):
    return lax.dot_general(a, b, (((1,), (1,)), ((), ())), preferred_element_type=F32)


def dot_tn(a, b):
    return lax.dot_general(a, b, (((0,), (0,)), ((), ())), preferred_element_type=F32)


def earlier_chunk():
    row = lax.broadcasted_iota(jnp.int32, (BLK, BLK), 0) // CH
    col = lax.broadcasted_iota(jnp.int32, (BLK, BLK), 1) // CH
    return row, col, col < row


def memory_kernel(rates_ref, kv_ref, total_ref, before_ref, inject_ref):
    blocks = kv_ref.shape[0]
    heads = total_ref.shape[0]
    row, col, strict = earlier_chunk()
    near = strict & (row // 2 == col // 2)
    middle = strict & (row // 4 == col // 4) & (row // 2 != col // 2)
    far = strict & (row // 4 != col // 4)
    eye = (
        lax.broadcasted_iota(jnp.int32, (BLK, BLK), 0)
        == lax.broadcasted_iota(jnp.int32, (BLK, BLK), 1)
    ).astype(F32)
    running = [jnp.concatenate([eye, jnp.zeros_like(eye)], axis=1) for _ in range(heads)]
    for b in range(blocks):
        for h in range(heads):
            rate = rates_ref[h]
            columns = pl.ds(h * BLK, BLK)
            k = kv_ref[b, 0, :, columns]
            v = kv_ref[b, 1, :, columns]
            kf = k.astype(F32)
            mean_square = jnp.mean(kf * kf, axis=-1, keepdims=True)
            norm = lax.rsqrt(BLK * (mean_square + 1e-06))
            across = jnp.broadcast_to(norm, (BLK, BLK))
            lower = dot_nt(k, k) * (across * across.T) * rate
            half = -jnp.where(near, lower, 0.0)
            inv = half + eye
            half = half - dot(inv, dot(jnp.where(middle, lower, 0.0), inv))
            inv = half + eye
            half = half - dot(inv, dot(jnp.where(far, lower, 0.0), inv))
            unit = kf * norm
            both = jnp.concatenate([unit, v.astype(F32)], axis=1)
            both = both + dot(half, both)
            weighted = (both * (norm * rate)).astype(BF16)
            inject_ref[h, b] = weighted
            change = dot_tn(k, weighted)
            shrink, offset = change[:, :BLK], change[:, BLK:]
            before = running[h].astype(BF16)
            before_ref[h, b] = before
            after = running[h] - dot(shrink, before)
            running[h] = jnp.concatenate([after[:, :BLK], after[:, BLK:] + offset], axis=1)
    for h in range(heads):
        total_ref[h] = running[h].astype(BF16)


def readout_kernel(q_ref, kv_ref, before_ref, inject_ref, lin_ref, off_ref):
    blocks = kv_ref.shape[0]
    heads = before_ref.shape[0]
    strict = earlier_chunk()[2]
    for b in range(blocks):
        for h in range(heads):
            columns = pl.ds(h * BLK, BLK)
            q = q_ref[b, :, columns]
            inner = jnp.where(strict, dot_nt(q, kv_ref[b, 0, :, columns]), 0.0)
            inside = dot(inner, inject_ref[h, b])
            rows = dot(q.astype(F32) - inside[:, :BLK], before_ref[h, b])
            lin_ref[h, b] = rows[:, :BLK].astype(BF16)
            off_ref[h, b] = rows[:, BLK:] + inside[:, BLK:]


def gate_kernel(first_ref, q_ref, far_ref, near_ref, state_ref, lin_ref, off_ref, out_ref):
    blocks = near_ref.shape[0]
    reach = far_ref.shape[0]
    heads = lin_ref.shape[0]
    row = lax.broadcasted_iota(jnp.int32, (BLK, BLK), 0)
    col = lax.broadcasted_iota(jnp.int32, (BLK, BLK), 1)
    scale = math.log2(math.e) / math.sqrt(BLK)
    for b in range(blocks):
        for h in range(heads):
            columns = pl.ds(h * BLK, BLK)
            q = q_ref[b, :, columns]
            spans = [(far_ref, c, False) for c in range(b, reach)]
            spans += [(near_ref, c, True) for c in range(max(0, b + 1 - reach), b + 1)]
            scores = []
            for ref, c, own in spans:
                s = dot_nt(q, ref[c, 0, :, columns])
                if own:
                    if c == b:
                        s = jnp.where(col <= row, s, MASKED)
                else:
                    keep = c >= first_ref[0]
                    if c == b:
                        s = jnp.where((col > row) & keep, s, MASKED)
                    else:
                        s = jnp.where(keep, s, MASKED)
                scores.append(s)
            s = jnp.concatenate(scores, axis=1)
            top = jnp.max(s, axis=-1, keepdims=True)
            p = jnp.exp2((s - top) * scale)
            total = jnp.sum(p, axis=-1, keepdims=True)
            p = p.astype(BF16)
            v = jnp.concatenate([ref[c, 1, :, columns] for ref, c, _ in spans], axis=0)
            attended = jnp.dot(p, v, preferred_element_type=F32) / total
            read = dot(lin_ref[h, b], state_ref[h]) + off_ref[h, b]
            out_ref[b, :, columns] = (attended * jax.nn.sigmoid(read)).astype(BF16)


def project_kernel(x_ref, w_ref, out_ref):
    acc = jnp.zeros(out_ref.shape, F32)
    for j in range(x_ref.shape[0]):
        acc += jnp.dot(x_ref[j], w_ref[j], preferred_element_type=F32)
    out_ref[...] = acc.astype(out_ref.dtype)


def vmem(count):
    return [pl.BlockSpec(memory_space=pltpu.VMEM)] * count


PARAMS = pltpu.CompilerParams(vmem_limit_bytes=48 * 1024 * 1024)


def compose(later, earlier):
    lin = jnp.einsum(
        "hij,hjk->hik", later[:, :, :BLK], earlier, precision=lax.Precision.HIGHEST
    )
    return lin + jnp.pad(later[:, :, BLK:], ((0, 0), (0, 0), (lin.shape[2] - BLK, 0)))


def states_at_start(total, init, groups, group_size):
    axis = "seq"
    group = lax.axis_index(axis) // group_size

    def shift(x, distance):
        route = [
            (i, i + distance * group_size) for i in range((groups - distance) * group_size)
        ]
        return lax.ppermute(x, axis, route)

    state = init
    if groups == 1:
        return state
    held = shift(total, 1).astype(F32)
    total = total.astype(F32)
    state = jnp.where(group == 1, compose(held, init), state)
    distance = 2
    while distance < groups:
        known = group < distance
        after = compose(total, state)
        if 2 * distance >= groups:
            moved = shift(after.astype(BF16), distance).astype(F32)
            return jnp.where(known, state, compose(held, moved))
        plain = jnp.concatenate([jnp.zeros_like(after), after], axis=2)
        sent = jnp.where(known, plain, compose(total, held)).astype(BF16)
        held = jnp.where(known, held, compose(held, shift(sent, distance).astype(F32)))
        solved = (group >= distance) & (group < 2 * distance)
        state = jnp.where(solved, held[:, :, BLK:], state)
        distance = 2 * distance
    return state


def shards(queries, keys, values, step_rate, memory_init, out_weight):
    axis = "seq"
    size = lax.axis_size(axis)
    place = lax.axis_index(axis)
    tokens, _ = queries.shape
    local_heads = memory_init.shape[0]
    group_size = math.gcd(local_heads, size, WIN // tokens)
    groups = size // group_size
    heads = local_heads // group_size
    width = heads * BLK
    span = tokens * group_size
    blocks = span // BLK
    reach = WIN // BLK
    members = [[g * group_size + i for i in range(group_size)] for g in range(groups)]

    def by_heads(x):
        parts = jnp.stack(x) if isinstance(x, tuple) else x[None]
        parts = parts.reshape(parts.shape[0], tokens, group_size, width).transpose(2, 0, 1, 3)
        if group_size > 1:
            parts = lax.all_to_all(parts, axis, 0, 0, axis_index_groups=members, tiled=True)
        return parts

    kv = by_heads((keys, values))
    q = by_heads(queries)
    if tokens != BLK:
        split = tokens // BLK
        kv = kv.reshape(group_size, 2, split, BLK, width).transpose(0, 2, 1, 3, 4)
        kv = kv.reshape(blocks, 2, BLK, width)
        q = q.reshape(blocks, 1, BLK, width)
    q = q[:, 0]
    far = []
    for distance in range(WIN // span, 0, -1):
        route = [(i, i + distance * group_size) for i in range(size - distance * group_size)]
        far.append(lax.ppermute(kv, axis, route))
    far = far[0] if len(far) == 1 else jnp.concatenate(far)

    member = place % group_size
    group = place // group_size
    rates = lax.dynamic_slice_in_dim(step_rate, member * heads, heads)
    init = lax.dynamic_slice_in_dim(memory_init, member * heads, heads)

    total, before, inject = pl.pallas_call(
        memory_kernel,
        out_shape=(
            jax.ShapeDtypeStruct((heads, BLK, 2 * BLK), BF16),
            jax.ShapeDtypeStruct((heads, blocks, BLK, 2 * BLK), BF16),
            jax.ShapeDtypeStruct((heads, blocks, BLK, 2 * BLK), BF16),
        ),
        in_specs=[pl.BlockSpec(memory_space=pltpu.SMEM)] + vmem(1),
        out_specs=tuple(vmem(3)),
        compiler_params=PARAMS,
        name="memory_updates",
    )(rates, kv)
    state = states_at_start(total, init, groups, group_size)
    lin, off = pl.pallas_call(
        readout_kernel,
        out_shape=(
            jax.ShapeDtypeStruct((heads, blocks, BLK, BLK), BF16),
            jax.ShapeDtypeStruct((heads, blocks, BLK, BLK), F32),
        ),
        in_specs=vmem(4),
        out_specs=tuple(vmem(2)),
        compiler_params=PARAMS,
        name="memory_readout",
    )(q, kv, before, inject)
    first = jnp.maximum(0, reach - group * blocks).astype(jnp.int32).reshape(1)
    gated = pl.pallas_call(
        gate_kernel,
        out_shape=jax.ShapeDtypeStruct((blocks, BLK, width), BF16),
        in_specs=[pl.BlockSpec(memory_space=pltpu.SMEM)] + vmem(6),
        out_specs=pl.BlockSpec(memory_space=pltpu.VMEM),
        compiler_params=PARAMS,
        name="attend_and_gate",
    )(first, q, far, kv, state, lin, off)
    gated = gated.reshape(group_size, tokens, width)
    if group_size > 1:
        gated = lax.all_to_all(gated, axis, 0, 0, axis_index_groups=members, tiled=True)
    features = out_weight.shape[1]
    split_out = lax.axis_size("tp") > 1
    tile = math.gcd(features, 512)
    projected = pl.pallas_call(
        project_kernel,
        grid=(features // tile,),
        out_shape=jax.ShapeDtypeStruct((tokens, features), F32 if split_out else BF16),
        in_specs=[
            pl.BlockSpec((group_size, tokens, width), lambda i: (0, 0, 0)),
            pl.BlockSpec((group_size, width, tile), lambda i: (0, 0, i)),
        ],
        out_specs=pl.BlockSpec((tokens, tile), lambda i: (0, i)),
        compiler_params=PARAMS,
        name="project",
    )(gated, out_weight.reshape(group_size, width, features))
    if split_out:
        projected = lax.psum_scatter(projected, "tp", scatter_dimension=1, tiled=True)
    return projected.astype(BF16)


def solution(mesh):
    return jax.shard_map(
        shards,
        mesh=mesh,
        in_specs=(
            P("seq", "tp"),
            P("seq", "tp"),
            P("seq", "tp"),
            P("tp"),
            P("tp", None, None),
            P("tp", None),
        ),
        out_specs=P("seq", "tp"),
        check_vma=False,
    )
```

```python
import functools
import math

import jax
import jax.numpy as jnp
from jax import lax
from jax.experimental import pallas as pl
from jax.experimental.pallas import tpu as pltpu
from jax.sharding import PartitionSpec as P

WIN = 1024
CH = 16
BLK = 128
MASKED = -1e30
BATCH = 8
SCALE = math.log2(math.e) / math.sqrt(BLK)
F32 = jnp.float32
BF16 = jnp.bfloat16


def dot(a, b):
    return jnp.dot(a.astype(BF16), b.astype(BF16), preferred_element_type=F32)


def dot_nt(a, b):
    return lax.dot_general(a, b, (((1,), (1,)), ((), ())), preferred_element_type=F32)


def dot_tn(a, b):
    return lax.dot_general(a, b, (((0,), (0,)), ((), ())), preferred_element_type=F32)


def earlier_chunk():
    row = lax.broadcasted_iota(jnp.int32, (BLK, BLK), 0) // CH
    col = lax.broadcasted_iota(jnp.int32, (BLK, BLK), 1) // CH
    return row, col, col < row


def head_columns(member, j, width):
    return pl.ds(pl.multiple_of(lax.bitwise_xor(member, 2 * j) * width, width), width)


def pick_kernel(where_ref, k_ref, v_ref, out_ref, sem):
    loads = []
    for j in range(out_ref.shape[0]):
        columns = head_columns(where_ref[0], j, out_ref.shape[-1])
        for t, source in enumerate((k_ref, v_ref)):
            loads.append(pltpu.make_async_copy(source.at[:, columns], out_ref.at[j, t], sem))
            loads[-1].start()
    wait_all(loads)


def pair_kernel(where_ref, mine_ref, k_ref, v_ref, *refs):
    outs, sem = refs[:-1], refs[-1]
    row = where_ref[0] & 1
    loads = []
    for j, out in enumerate(outs):
        columns = head_columns(where_ref[0], j, out.shape[-1])
        for t, source in enumerate((k_ref, v_ref)):
            loads.append(pltpu.make_async_copy(source.at[:, columns], out.at[1 - row, t], sem))
            loads[-1].start()
    for j, out in enumerate(outs):
        out[pl.ds(row, 1)] = mine_ref[j : j + 1]
    wait_all(loads)


def pair_queries_kernel(where_ref, mine_ref, theirs_ref, *refs):
    outs, sem = refs[-5:-1], refs[-1]
    row = where_ref[0] & 1
    loads = []
    for j, out in enumerate(outs):
        columns = head_columns(where_ref[0], j, out.shape[-1])
        for i, source in enumerate((mine_ref, theirs_ref)):
            loads.append(pltpu.make_async_copy(source.at[:, columns], out.at[row ^ i], sem))
            loads[-1].start()
    wait_all(loads)


def place_pieces(layout, member, pieces, held_ref):
    for piece, index, count, number in layout:
        held_ref[pl.ds(number(member), count)] = pieces[piece][index : index + count]


def wait_all(copies):
    for copy in copies:
        copy.wait()


def memory_kernel(layout, where_ref, rates_ref, *refs):
    pieces, (total_ref, before_out, inject_out) = refs[:-8], refs[-8:-5]
    shrink_ref, offset_ref, before_ref, inject_ref, sem = refs[-5:]
    blocks = before_ref.shape[0]
    heads = total_ref.shape[0]
    numbers, sources = [], []
    for piece, index, count, number in layout:
        numbers += [number(where_ref[0]) + i for i in range(count)]
        sources += [(pieces[piece], index + i) for i in range(count)]
    row, col, strict = earlier_chunk()
    near = strict & (row // 2 == col // 2)
    middle = strict & (row // 4 == col // 4) & (row // 2 != col // 2)
    far = strict & (row // 4 != col // 4)
    eye = (
        lax.broadcasted_iota(jnp.int32, (BLK, BLK), 0)
        == lax.broadcasted_iota(jnp.int32, (BLK, BLK), 1)
    ).astype(F32)
    todo = [(p, h) for p in range(blocks) for h in range(heads)]
    every = range(len(todo))
    rate = [rates_ref[where_ref[0] * heads + h] for _, h in todo]
    k, v = [
        [sources[p][0][sources[p][1], t, :, h * BLK : (h + 1) * BLK] for p, h in todo]
        for t in range(2)
    ]
    kf = [x.astype(F32) for x in k]
    norm = [
        lax.rsqrt(BLK * (jnp.mean(x * x, axis=-1, keepdims=True) + 1e-06)) for x in kf
    ]
    unit = [kf[i] * norm[i] for i in every]
    rounded = [x.astype(BF16) for x in unit]
    lower = [dot_nt(rounded[i], rounded[i]) * rate[i] for i in every]
    half = [-jnp.where(near, x, 0.0) for x in lower]
    for region in (middle, far):
        inv = [(x + eye).astype(BF16) for x in half]
        part = [dot(jnp.where(region, lower[i], 0.0), inv[i]) for i in every]
        half = [half[i] - dot(inv[i], part[i]) for i in every]
    both = [dot(half[i], jnp.concatenate([rounded[i], v[i]], axis=1)) for i in every]
    both = [
        both[i] + jnp.concatenate([unit[i], v[i].astype(F32)], axis=1) for i in every
    ]
    weighted = [(both[i] * (norm[i] * rate[i])).astype(BF16) for i in every]
    for i, (p, h) in enumerate(todo):
        inject_ref[numbers[p], h] = weighted[i]
    stores = [pltpu.make_async_copy(inject_ref, inject_out, sem.at[0])]
    stores[0].start()
    change = [dot_tn(k[i], weighted[i]) for i in every]
    for i, (p, h) in enumerate(todo):
        shrink_ref[numbers[p], h] = change[i][:, :BLK].astype(BF16)
        offset_ref[numbers[p], h] = change[i][:, BLK:]
    running = [jnp.concatenate([eye, jnp.zeros_like(eye)], axis=1) for _ in range(heads)]
    for b in range(blocks):
        for h in range(heads):
            before = running[h].astype(BF16)
            before_ref[b, h] = before
            after = running[h] - dot(shrink_ref[b, h], before)
            running[h] = jnp.concatenate(
                [after[:, :BLK], after[:, BLK:] + offset_ref[b, h]], axis=1
            )
        stores.append(
            pltpu.make_async_copy(before_ref.at[b], before_out.at[b], sem.at[1])
        )
        stores[-1].start()
    for h in range(heads):
        total_ref[h] = running[h].astype(BF16)
    wait_all(stores)


def own_state(where_ref, init_hbm, init_ref, sem):
    heads = init_ref.shape[0]
    copy = pltpu.make_async_copy(init_hbm.at[pl.ds(where_ref[0] * heads, heads)], init_ref, sem)
    copy.start()
    return copy


def advance(update, state):
    return dot(update[:, :BLK], state) + update[:, BLK:].astype(F32)


def after_kernel(
    where_ref, held_ref, total_ref, init_hbm, _, __, own_ref, after_ref, init_ref, sem
):
    own_state(where_ref, init_hbm, init_ref, sem).wait()
    second = where_ref[1] % 2 == 1
    for h in range(after_ref.shape[0]):
        state = init_ref[h]
        earlier = advance(jnp.where(second, held_ref[h], total_ref[h]), state)
        own_ref[h] = jnp.where(second, earlier, state)
        later = jnp.where(second, total_ref[h], held_ref[h])
        after_ref[h] = advance(later, earlier).astype(BF16)


def chain_kernel(where_ref, updates_ref, init_hbm, state_ref, sem):
    own_state(where_ref, init_hbm, state_ref, sem).wait()

    @pl.loop(0, where_ref[1])
    def _(g):
        for h in range(state_ref.shape[0]):
            state_ref[h] = advance(updates_ref[g, h], state_ref[h])


def within_block():
    row = lax.broadcasted_iota(jnp.int32, (BLK, BLK), 0)
    col = lax.broadcasted_iota(jnp.int32, (BLK, BLK), 1)
    return row, col


def weigh(p, v):
    return jnp.dot(p, jnp.concatenate([v, jnp.ones_like(v)], axis=1), preferred_element_type=F32)


def batches(blocks, heads):
    todo = [(b, h) for b in range(blocks) for h in range(heads)]
    return [todo[i : i + BATCH] for i in range(0, len(todo), BATCH)]


def local_kernel(kv_layout, q_layout, where_ref, *refs):
    kv_pieces = refs[: len(kv_layout)]
    q_pieces = refs[len(kv_layout) : len(kv_layout) + len(q_layout)]
    before_hbm, inject_hbm = refs[len(kv_layout) + len(q_layout) :][:2]
    attended_ref, logs_ref, lin_ref, off_ref = refs[-9:-5]
    q_ref, kv_ref, before_ref, inject_ref, sem = refs[-5:]
    blocks = kv_ref.shape[0]
    heads = attended_ref.shape[0]
    late = [
        pltpu.make_async_copy(before_hbm, before_ref, sem.at[0]),
        pltpu.make_async_copy(inject_hbm, inject_ref, sem.at[1]),
    ]
    for copy in late:
        copy.start()
    place_pieces(q_layout, where_ref[0], q_pieces, q_ref)
    place_pieces(kv_layout, where_ref[0], kv_pieces, kv_ref)
    row, col = within_block()
    logs = [jnp.zeros((BLK, BLK), F32) for _ in range(heads)]
    for part in batches(blocks, heads):
        scores = []
        for b, h in part:
            columns = slice(h * BLK, (h + 1) * BLK)
            q = q_ref[b, :, columns]
            s = jnp.where(col <= row, dot_nt(q, kv_ref[b, 0, :, columns]), MASKED)
            if b > 0:
                k = kv_ref[0:b, 0, :, columns].reshape(b * BLK, BLK)
                s = jnp.concatenate([dot_nt(q, k), s], axis=1)
            scores.append(s)
        top = [jnp.max(s, axis=-1, keepdims=True) * SCALE for s in scores]
        p = [jnp.exp2(s * SCALE - t).astype(BF16) for s, t in zip(scores, top)]
        for i, (b, h) in enumerate(part):
            columns = slice(h * BLK, (h + 1) * BLK)
            v = kv_ref[0 : b + 1, 1, :, columns].reshape((b + 1) * BLK, BLK)
            acc = weigh(p[i], v)
            total = acc[:, BLK:]
            attended_ref[h, b] = acc[:, :BLK] / total
            logs[h] = jnp.where(col == b, jnp.log2(total) + top[i], logs[h])
    for h in range(heads):
        logs_ref[h] = logs[h]
    wait_all(late)
    strict = earlier_chunk()[2]
    todo = [(b, h) for b in range(blocks) for h in range(heads)]
    every = range(len(todo))
    q = [q_ref[b, :, h * BLK : (h + 1) * BLK] for b, h in todo]
    inner = [
        jnp.where(strict, dot_nt(q[i], kv_ref[b, 0, :, h * BLK : (h + 1) * BLK]), 0.0)
        for i, (b, h) in enumerate(todo)
    ]
    inside = [dot(inner[i], inject_ref[b, h]) for i, (b, h) in enumerate(todo)]
    rows = [
        dot(q[i].astype(F32) - inside[i][:, :BLK], before_ref[b, h])
        for i, (b, h) in enumerate(todo)
    ]
    for i, (b, h) in enumerate(todo):
        lin_ref[h, b] = rows[i][:, :BLK].astype(BF16)
        off_ref[h, b] = rows[i][:, BLK:] + inside[i][:, BLK:]


def far_kernel(layout, q_layout, where_ref, near_ref, logs_ref, *refs):
    pieces, q_pieces = refs[: len(layout)], refs[len(layout) : -3]
    out_ref, q_ref, kv_ref = refs[-3:]
    reach = kv_ref.shape[0]
    blocks = q_ref.shape[0]
    place_pieces(q_layout, where_ref[0], q_pieces, q_ref)
    place_pieces(layout, where_ref[0], pieces, kv_ref)
    row, col = within_block()
    hidden = [
        jnp.where(where_ref[1] * blocks + c < reach, MASKED, 0.0) for c in range(reach)
    ]
    for part in batches(blocks, near_ref.shape[0]):
        scores = []
        for b, h in part:
            columns = slice(h * BLK, (h + 1) * BLK)
            k = kv_ref[b:reach, 0, :, columns].reshape((reach - b) * BLK, BLK)
            s = dot_nt(q_ref[b, :, columns], k)
            s = [s[:, i * BLK : (i + 1) * BLK] + hidden[b + i] for i in range(reach - b)]
            s[0] = jnp.where(col > row, s[0], MASKED)
            scores.append(jnp.concatenate(s, axis=1) if len(s) > 1 else s[0])
        old = [logs_ref[h][:, b : b + 1] for b, h in part]
        top = [
            jnp.maximum(jnp.max(s, axis=-1, keepdims=True) * SCALE, t)
            for s, t in zip(scores, old)
        ]
        p = [jnp.exp2(s * SCALE - t).astype(BF16) for s, t in zip(scores, top)]
        kept = [jnp.exp2(o - t) for o, t in zip(old, top)]
        for i, (b, h) in enumerate(part):
            columns = slice(h * BLK, (h + 1) * BLK)
            v = kv_ref[b:reach, 1, :, columns].reshape((reach - b) * BLK, BLK)
            acc = weigh(p[i], v)
            sums = acc[:, :BLK] + near_ref[h, b] * kept[i]
            out_ref[h, b] = sums / (acc[:, BLK:] + kept[i])


def gate_kernel(where_ref, attended_ref, lin_ref, off_ref, own_ref, moved_ref, held_ref, *refs):
    outs = refs
    heads, blocks = lin_ref.shape[:2]
    count = blocks // len(outs)
    late = where_ref[1] > where_ref[2]
    odd = where_ref[1] % 2 == 1
    state = []
    for h in range(heads):
        moved = moved_ref[h].astype(F32)
        moved = jnp.where(odd, advance(held_ref[h], moved), moved)
        state.append(jnp.where(late, moved, own_ref[h]).astype(BF16))
    numbers = [lax.bitwise_xor(where_ref[0], s) * count for s in range(len(outs))]
    todo = [(s, i, h) for s in range(len(outs)) for i in range(count) for h in range(heads)]
    read = [
        dot(lin_ref[h, numbers[s] + i], state[h]) + off_ref[h, numbers[s] + i]
        for s, i, h in todo
    ]
    for (s, i, h), r in zip(todo, read):
        gated = attended_ref[h, numbers[s] + i] * jax.nn.sigmoid(r)
        rows = slice(i * BLK, (i + 1) * BLK)
        outs[s][rows, h * BLK : (h + 1) * BLK] = gated.astype(BF16)


def project_kernel(where_ref, w_ref, *refs):
    pieces, out_ref = refs[:-1], refs[-1]
    width = pieces[0].shape[1]
    acc = jnp.zeros(out_ref.shape, F32)
    for s, piece in enumerate(pieces):
        first = pl.multiple_of(lax.bitwise_xor(where_ref[0], s) * width, width)
        acc += jnp.dot(piece[...], w_ref[pl.ds(first, width), :], preferred_element_type=F32)
    out_ref[...] = acc.astype(out_ref.dtype)


VMEM = pl.BlockSpec(memory_space=pltpu.VMEM)
ANY = pl.BlockSpec(memory_space=pl.ANY)
HBM = pl.BlockSpec(memory_space=pltpu.HBM)
SMEM = pl.BlockSpec(memory_space=pltpu.SMEM)


def params(mebibytes):
    return pltpu.CompilerParams(vmem_limit_bytes=mebibytes * 1024 * 1024)


def cost(flops, moved):
    return pl.CostEstimate(flops=flops, bytes_accessed=moved, transcendentals=0)


def shape(dims, kind):
    return jax.ShapeDtypeStruct(dims, kind)


def shards(queries, keys, values, step_rate, memory_init, out_weight):
    axis = "seq"
    size = lax.axis_size(axis)
    place = lax.axis_index(axis).astype(jnp.int32)
    tokens, _ = queries.shape
    local_heads = memory_init.shape[0]
    group_size = math.gcd(local_heads, size, WIN // tokens)
    groups = size // group_size
    heads = local_heads // group_size
    width = heads * BLK
    span = tokens * group_size
    blocks = span // BLK
    reach = WIN // BLK
    members = [[g * group_size + i for i in range(group_size)] for g in range(groups)]
    member = place % group_size
    group = place // group_size
    direct = group_size == 8 and span == WIN and tokens == BLK and groups == 4

    def flip(x, mask):
        return lax.ppermute(x, axis, [(i, i ^ mask) for i in range(size)])

    def onward(x, distance):
        shift = distance * group_size
        return lax.ppermute(x, axis, [(i, i + shift) for i in range(size - shift)])

    last_own = 1 if direct else groups
    where = jnp.stack([member, group, jnp.int32(last_own)])
    dma = pltpu.SemaphoreType.DMA

    if direct:
        *theirs, their_queries = [flip(x, 1) for x in (keys, values, queries)]
        mine = pl.pallas_call(
            pick_kernel,
            out_shape=shape((4, 2, BLK, width), BF16),
            in_specs=[SMEM] + [ANY] * 2,
            out_specs=VMEM,
            scratch_shapes=[dma],
            compiler_params=params(4),
            cost_estimate=cost(1, 1),
            name="pick",
        )(where, keys, values)
        sent = pl.pallas_call(
            pair_kernel,
            out_shape=[shape((2, 2, BLK, width), BF16)] * 4,
            in_specs=[SMEM, VMEM] + [ANY] * 2,
            out_specs=[VMEM] * 4,
            scratch_shapes=[dma],
            compiler_params=params(4),
            cost_estimate=cost(1, 1),
            name="pair",
        )(where, mine, *theirs)
        kv = [sent[0]] + [flip(sent[j], 2 * j) for j in range(1, 4)]
        layout = [(j, 0, 2, lambda m, j=j: (m ^ (2 * j)) // 2 * 2) for j in range(4)]
        q_layout = far_layout = layout
        far = [onward(x, 1) for x in kv]
        ready = far[1:2]
        q = pl.pallas_call(
            pair_queries_kernel,
            out_shape=[shape((2, BLK, width), BF16)] * 4,
            in_specs=[SMEM] + [ANY] * 4,
            out_specs=[VMEM] * 4,
            scratch_shapes=[dma],
            compiler_params=params(4),
            cost_estimate=cost(1, 1),
            name="pair_queries",
        )(where, queries, their_queries, kv[3], far[0])
        q = [q[0]] + [flip(q[j], 2 * j) for j in range(1, 4)]
    else:

        def by_heads(parts):
            parts = parts.reshape(-1, tokens // BLK, BLK, group_size, width)
            parts = parts.transpose(3, 1, 0, 2, 4)
            if group_size > 1:
                parts = lax.all_to_all(parts, axis, 0, 0, axis_index_groups=members, tiled=True)
            return parts.reshape(blocks, -1, BLK, width)

        kv = [by_heads(jnp.stack([keys, values]))]
        q = [by_heads(queries)[:, 0]]
        far = [onward(kv[0], distance) for distance in range(WIN // span, 0, -1)]
        layout = q_layout = [(0, 0, blocks, lambda m: 0)]
        ready = []
        far_layout = [(c, 0, blocks, lambda m, c=c: c * blocks) for c in range(len(far))]

    total, before, inject = pl.pallas_call(
        functools.partial(memory_kernel, layout),
        out_shape=[
            shape((heads, BLK, 2 * BLK), BF16),
            shape((blocks, heads, BLK, 2 * BLK), BF16),
            shape((blocks, heads, BLK, 2 * BLK), BF16),
        ],
        in_specs=[SMEM, SMEM] + [VMEM] * len(kv),
        out_specs=[VMEM, HBM, HBM],
        scratch_shapes=[
            pltpu.VMEM((blocks, heads, BLK, BLK), BF16),
            pltpu.VMEM((blocks, heads, BLK, BLK), F32),
            pltpu.VMEM((blocks, heads, BLK, 2 * BLK), BF16),
            pltpu.VMEM((blocks, heads, BLK, 2 * BLK), BF16),
            dma((2,)),
        ],
        compiler_params=params(12),
        cost_estimate=cost(1, 1),
        name="memory_updates",
    )(where, step_rate, *kv)

    state_shape = shape((heads, BLK, BLK), F32)
    near, logs, lin, off = pl.pallas_call(
        functools.partial(local_kernel, layout, q_layout),
        out_shape=[
            shape((heads, blocks, BLK, BLK), F32),
            state_shape,
            shape((heads, blocks, BLK, BLK), BF16),
            shape((heads, blocks, BLK, BLK), F32),
        ],
        in_specs=[SMEM] + [VMEM] * (len(kv) + len(q)) + [HBM] * 2 + [ANY] * len(ready),
        out_specs=[VMEM] * 4,
        scratch_shapes=[
            pltpu.VMEM((blocks, BLK, width), BF16),
            pltpu.VMEM((blocks, 2, BLK, width), BF16),
            pltpu.VMEM((blocks, heads, BLK, 2 * BLK), BF16),
            pltpu.VMEM((blocks, heads, BLK, 2 * BLK), BF16),
            dma((2,)),
        ],
        compiler_params=params(12),
        cost_estimate=cost(4 * 10**9, 1),
        name="attend_own",
    )(where, *kv, *q, before, inject, *ready)
    if direct:
        held = flip(total, group_size)
        own, after = pl.pallas_call(
            after_kernel,
            out_shape=[state_shape, shape((heads, BLK, BLK), BF16)],
            in_specs=[SMEM, VMEM, VMEM, HBM, ANY, ANY],
            out_specs=[VMEM, VMEM],
            scratch_shapes=[pltpu.VMEM((heads, BLK, BLK), F32), dma],
            compiler_params=params(8),
            cost_estimate=cost(1, 1),
            name="state_after",
        )(where, held, total, memory_init, logs, far[2])
        moved = flip(after, 2 * group_size)
    else:
        updates = lax.all_gather(
            total, axis, axis_index_groups=[list(x) for x in zip(*members)]
        )
        own = pl.pallas_call(
            chain_kernel,
            out_shape=state_shape,
            in_specs=[SMEM, VMEM, HBM],
            out_specs=VMEM,
            scratch_shapes=[dma],
            compiler_params=params(32),
            name="state_chain",
        )(where, updates, memory_init)
        moved, held = own.astype(BF16), total

    attended = pl.pallas_call(
        functools.partial(far_kernel, far_layout, q_layout),
        out_shape=shape((heads, blocks, BLK, BLK), F32),
        in_specs=[SMEM] + [VMEM] * (2 + len(far) + len(q)),
        out_specs=VMEM,
        scratch_shapes=[
            pltpu.VMEM((blocks, BLK, width), BF16),
            pltpu.VMEM((reach, 2, BLK, width), BF16),
        ],
        compiler_params=params(12),
        cost_estimate=cost(4 * 10**9, 1),
        name="attend_far",
    )(where, near, logs, *far, *q)
    gated = pl.pallas_call(
        gate_kernel,
        out_shape=[shape((tokens, width), BF16)] * group_size,
        in_specs=[SMEM] + [VMEM] * 6,
        out_specs=[VMEM] * group_size,
        compiler_params=params(8),
        cost_estimate=cost(10**9, 1),
        name="gate",
    )(where, attended, lin, off, own, moved, held)
    gated = [gated[0]] + [flip(gated[s], s) for s in range(1, group_size)]
    features = out_weight.shape[1]
    split_out = lax.axis_size("tp") > 1
    projected = pl.pallas_call(
        project_kernel,
        out_shape=shape((tokens, features), F32 if split_out else BF16),
        in_specs=[SMEM] + [VMEM] * (1 + group_size),
        out_specs=VMEM,
        compiler_params=params(8),
        name="project",
    )(where, out_weight, *gated)
    if split_out:
        projected = lax.psum_scatter(projected, "tp", scatter_dimension=1, tiled=True)
    return projected.astype(BF16)


def solution(mesh):
    return jax.shard_map(
        shards,
        mesh=mesh,
        in_specs=(
            P("seq", "tp"),
            P("seq", "tp"),
            P("seq", "tp"),
            P("tp"),
            P("tp", None, None),
            P("tp", None),
        ),
        out_specs=P("seq", "tp"),
        check_vma=False,
    )
```

```python
import functools
import math

import jax
import jax.numpy as jnp
from jax import lax
from jax.experimental import pallas as pl
from jax.experimental.pallas import tpu as pltpu
from jax.sharding import PartitionSpec as P

WIN = 1024
CH = 16
BLK = 128
MASKED = -1e30
BATCH = 8
SCALE = math.log2(math.e) / math.sqrt(BLK)
F32 = jnp.float32
BF16 = jnp.bfloat16


def dot(a, b):
    return jnp.dot(a.astype(BF16), b.astype(BF16), preferred_element_type=F32)


def dot_nt(a, b):
    return lax.dot_general(a, b, (((1,), (1,)), ((), ())), preferred_element_type=F32)


def dot_tn(a, b):
    return lax.dot_general(a, b, (((0,), (0,)), ((), ())), preferred_element_type=F32)


def earlier_chunk():
    row = lax.broadcasted_iota(jnp.int32, (BLK, BLK), 0) // CH
    col = lax.broadcasted_iota(jnp.int32, (BLK, BLK), 1) // CH
    return row, col, col < row


def head_columns(member, j, width):
    return pl.ds(pl.multiple_of(lax.bitwise_xor(member, 2 * j) * width, width), width)


def pick_kernel(where_ref, k_ref, v_ref, out_ref):
    for j in range(out_ref.shape[0]):
        columns = head_columns(where_ref[0], j, out_ref.shape[-1])
        out_ref[j, 0] = k_ref[:, columns]
        out_ref[j, 1] = v_ref[:, columns]


def pair_kernel(where_ref, mine_ref, k_ref, v_ref, *outs):
    row = where_ref[0] & 1
    for j, out in enumerate(outs):
        columns = head_columns(where_ref[0], j, out.shape[-1])
        out[pl.ds(row, 1)] = mine_ref[j : j + 1]
        out[pl.ds(1 - row, 1), 0] = k_ref[:, columns][None]
        out[pl.ds(1 - row, 1), 1] = v_ref[:, columns][None]


def pair_queries_kernel(where_ref, mine_ref, theirs_ref, _, *outs):
    row = where_ref[0] & 1
    for j, out in enumerate(outs):
        columns = head_columns(where_ref[0], j, out.shape[-1])
        out[pl.ds(row, 1)] = mine_ref[:, columns][None]
        out[pl.ds(1 - row, 1)] = theirs_ref[:, columns][None]


def join_kernel(*refs):
    pieces, out_ref = refs[:-1], refs[-1]
    for i, piece in enumerate(pieces):
        count = piece.shape[0]
        out_ref[i * count : (i + 1) * count] = piece[...]


def place_pieces(layout, member, pieces, held_ref):
    for piece, index, count, number in layout:
        held_ref[pl.ds(number(member), count)] = pieces[piece][index : index + count]


def wait_all(copies):
    for copy in copies:
        copy.wait()


def memory_kernel(layout, where_ref, rates_ref, *refs):
    pieces, (total_ref, before_ref, inject_ref, kv_ref) = refs[:-4], refs[-4:]
    blocks = before_ref.shape[0]
    heads = total_ref.shape[0]
    place_pieces(layout, where_ref[0], pieces, kv_ref)
    row, col, strict = earlier_chunk()
    near = strict & (row // 2 == col // 2)
    middle = strict & (row // 4 == col // 4) & (row // 2 != col // 2)
    far = strict & (row // 4 != col // 4)
    eye = (
        lax.broadcasted_iota(jnp.int32, (BLK, BLK), 0)
        == lax.broadcasted_iota(jnp.int32, (BLK, BLK), 1)
    ).astype(F32)
    todo = [(b, h) for b in range(blocks) for h in range(heads)]
    every = range(len(todo))
    rate = [rates_ref[h] for _, h in todo]
    k, v = [
        [kv_ref[b, t, :, h * BLK : (h + 1) * BLK] for b, h in todo]
        for t in range(2)
    ]
    kf = [x.astype(F32) for x in k]
    norm = [
        lax.rsqrt(BLK * (jnp.mean(x * x, axis=-1, keepdims=True) + 1e-06)) for x in kf
    ]
    unit = [kf[i] * norm[i] for i in every]
    rounded = [x.astype(BF16) for x in unit]
    lower = [dot_nt(rounded[i], rounded[i]) * rate[i] for i in every]
    half = [-jnp.where(near, x, 0.0) for x in lower]
    for region in (middle, far):
        inv = [(x + eye).astype(BF16) for x in half]
        part = [dot(jnp.where(region, lower[i], 0.0), inv[i]) for i in every]
        half = [half[i] - dot(inv[i], part[i]) for i in every]
    both = [dot(half[i], jnp.concatenate([rounded[i], v[i]], axis=1)) for i in every]
    both = [
        both[i] + jnp.concatenate([unit[i], v[i].astype(F32)], axis=1) for i in every
    ]
    weighted = [(both[i] * (norm[i] * rate[i])).astype(BF16) for i in every]
    for i, (b, h) in enumerate(todo):
        inject_ref[b, h] = weighted[i]
    change = [dot_tn(k[i], weighted[i]) for i in every]
    running = [jnp.concatenate([eye, jnp.zeros_like(eye)], axis=1) for _ in range(heads)]
    for i, (b, h) in enumerate(todo):
        before = running[h].astype(BF16)
        before_ref[b, h] = before
        after = running[h] - dot(change[i][:, :BLK], before)
        running[h] = jnp.concatenate(
            [after[:, :BLK], after[:, BLK:] + change[i][:, BLK:]], axis=1
        )
    for h in range(heads):
        total_ref[h] = running[h].astype(BF16)


def own_state(where_ref, init_hbm, init_ref, sem):
    heads = init_ref.shape[0]
    copy = pltpu.make_async_copy(init_hbm.at[pl.ds(where_ref[0] * heads, heads)], init_ref, sem)
    copy.start()
    return copy


def advance(update, state):
    return dot(update[:, :BLK], state) + update[:, BLK:].astype(F32)


def after_kernel(
    where_ref, held_ref, total_ref, init_hbm, _, __, own_ref, after_ref, init_ref, sem
):
    own_state(where_ref, init_hbm, init_ref, sem).wait()
    second = where_ref[1] % 2 == 1
    for h in range(after_ref.shape[0]):
        state = init_ref[h]
        earlier = advance(jnp.where(second, held_ref[h], total_ref[h]), state)
        own_ref[h] = jnp.where(second, earlier, state)
        later = jnp.where(second, total_ref[h], held_ref[h])
        after_ref[h] = advance(later, earlier).astype(BF16)


def chain_kernel(where_ref, updates_ref, init_hbm, state_ref, sem):
    own_state(where_ref, init_hbm, state_ref, sem).wait()

    @pl.loop(0, where_ref[1])
    def _(g):
        for h in range(state_ref.shape[0]):
            state_ref[h] = advance(updates_ref[g, h], state_ref[h])


def within_block():
    row = lax.broadcasted_iota(jnp.int32, (BLK, BLK), 0)
    col = lax.broadcasted_iota(jnp.int32, (BLK, BLK), 1)
    return row, col


def weigh(p, v):
    return jnp.dot(p, jnp.concatenate([v, jnp.ones_like(v)], axis=1), preferred_element_type=F32)


def batches(blocks, heads):
    todo = [(b, h) for b in range(blocks) for h in range(heads)]
    return [todo[i : i + BATCH] for i in range(0, len(todo), BATCH)]


def local_kernel(kv_layout, q_layout, where_ref, *refs):
    kv_pieces = refs[: len(kv_layout)]
    q_pieces = refs[len(kv_layout) : len(kv_layout) + len(q_layout)]
    before_ref, inject_ref, attended_ref, logs_ref, lin_ref, off_ref, q_ref, kv_ref = refs[-8:]
    blocks = kv_ref.shape[0]
    heads = attended_ref.shape[0]
    place_pieces(q_layout, where_ref[0], q_pieces, q_ref)
    place_pieces(kv_layout, where_ref[0], kv_pieces, kv_ref)
    row, col = within_block()
    logs = [jnp.zeros((BLK, BLK), F32) for _ in range(heads)]
    for part in batches(blocks, heads):
        scores = []
        for b, h in part:
            columns = slice(h * BLK, (h + 1) * BLK)
            q = q_ref[b, :, columns]
            s = jnp.where(col <= row, dot_nt(q, kv_ref[b, 0, :, columns]), MASKED)
            if b > 0:
                k = kv_ref[0:b, 0, :, columns].reshape(b * BLK, BLK)
                s = jnp.concatenate([dot_nt(q, k), s], axis=1)
            scores.append(s)
        top = [jnp.max(s, axis=-1, keepdims=True) * SCALE for s in scores]
        p = [jnp.exp2(s * SCALE - t).astype(BF16) for s, t in zip(scores, top)]
        for i, (b, h) in enumerate(part):
            columns = slice(h * BLK, (h + 1) * BLK)
            v = kv_ref[0 : b + 1, 1, :, columns].reshape((b + 1) * BLK, BLK)
            acc = weigh(p[i], v)
            total = acc[:, BLK:]
            attended_ref[h, b] = acc[:, :BLK] / total
            logs[h] = jnp.where(col == b, jnp.log2(total) + top[i], logs[h])
    for h in range(heads):
        logs_ref[h] = logs[h]
    strict = earlier_chunk()[2]
    todo = [(b, h) for b in range(blocks) for h in range(heads)]
    every = range(len(todo))
    q = [q_ref[b, :, h * BLK : (h + 1) * BLK] for b, h in todo]
    inner = [
        jnp.where(strict, dot_nt(q[i], kv_ref[b, 0, :, h * BLK : (h + 1) * BLK]), 0.0)
        for i, (b, h) in enumerate(todo)
    ]
    inside = [dot(inner[i], inject_ref[b, h]) for i, (b, h) in enumerate(todo)]
    rows = [
        dot(q[i].astype(F32) - inside[i][:, :BLK], before_ref[b, h])
        for i, (b, h) in enumerate(todo)
    ]
    for i, (b, h) in enumerate(todo):
        lin_ref[h, b] = rows[i][:, :BLK].astype(BF16)
        off_ref[h, b] = rows[i][:, BLK:] + inside[i][:, BLK:]


def far_kernel(layout, q_layout, where_ref, near_ref, logs_ref, *refs):
    pieces, q_pieces = refs[: -3 - len(q_layout)], refs[-3 - len(q_layout) : -3]
    out_ref, q_ref, kv_ref = refs[-3:]
    reach = kv_ref.shape[0]
    blocks = q_ref.shape[0]
    place_pieces(q_layout, where_ref[0], q_pieces, q_ref)
    place_pieces(layout, where_ref[0], pieces, kv_ref)
    row, col = within_block()
    hidden = [
        jnp.where(where_ref[1] * blocks + c < reach, MASKED, 0.0) for c in range(reach)
    ]
    for part in batches(blocks, near_ref.shape[0]):
        scores = []
        for b, h in part:
            columns = slice(h * BLK, (h + 1) * BLK)
            k = kv_ref[b:reach, 0, :, columns].reshape((reach - b) * BLK, BLK)
            s = dot_nt(q_ref[b, :, columns], k)
            s = [s[:, i * BLK : (i + 1) * BLK] + hidden[b + i] for i in range(reach - b)]
            s[0] = jnp.where(col > row, s[0], MASKED)
            scores.append(jnp.concatenate(s, axis=1) if len(s) > 1 else s[0])
        old = [logs_ref[h][:, b : b + 1] for b, h in part]
        top = [
            jnp.maximum(jnp.max(s, axis=-1, keepdims=True) * SCALE, t)
            for s, t in zip(scores, old)
        ]
        p = [jnp.exp2(s * SCALE - t).astype(BF16) for s, t in zip(scores, top)]
        kept = [jnp.exp2(o - t) for o, t in zip(old, top)]
        for i, (b, h) in enumerate(part):
            columns = slice(h * BLK, (h + 1) * BLK)
            v = kv_ref[b:reach, 1, :, columns].reshape((reach - b) * BLK, BLK)
            acc = weigh(p[i], v)
            sums = acc[:, :BLK] + near_ref[h, b] * kept[i]
            out_ref[h, b] = sums / (acc[:, BLK:] + kept[i])


def gate_kernel(where_ref, attended_ref, lin_ref, off_ref, own_ref, moved_ref, held_ref, *refs):
    outs = refs
    heads, blocks = lin_ref.shape[:2]
    count = blocks // len(outs)
    late = where_ref[1] > where_ref[2]
    odd = where_ref[1] % 2 == 1
    state = []
    for h in range(heads):
        moved = moved_ref[h].astype(F32)
        moved = jnp.where(odd, advance(held_ref[h], moved), moved)
        state.append(jnp.where(late, moved, own_ref[h]).astype(BF16))
    numbers = [lax.bitwise_xor(where_ref[0], s) * count for s in range(len(outs))]
    todo = [(s, i, h) for s in range(len(outs)) for i in range(count) for h in range(heads)]
    read = [
        dot(lin_ref[h, numbers[s] + i], state[h]) + off_ref[h, numbers[s] + i]
        for s, i, h in todo
    ]
    for (s, i, h), r in zip(todo, read):
        gated = attended_ref[h, numbers[s] + i] * jax.nn.sigmoid(r)
        rows = slice(i * BLK, (i + 1) * BLK)
        outs[s][rows, h * BLK : (h + 1) * BLK] = gated.astype(BF16)


def project_kernel(place, where_ref, w_ref, *refs):
    pieces, (*before, out_ref) = refs[: len(place)], refs[len(place) :]
    width = pieces[0].shape[1]
    acc = before[0][...] if before else jnp.zeros(out_ref.shape, F32)
    for s, piece in zip(place, pieces):
        first = pl.multiple_of(lax.bitwise_xor(where_ref[0], s) * width, width)
        acc += jnp.dot(piece[...], w_ref[pl.ds(first, width), :], preferred_element_type=F32)
    out_ref[...] = acc.astype(out_ref.dtype)


VMEM = pl.BlockSpec(memory_space=pltpu.VMEM)
ANY = pl.BlockSpec(memory_space=pl.ANY)
HBM = pl.BlockSpec(memory_space=pltpu.HBM)
SMEM = pl.BlockSpec(memory_space=pltpu.SMEM)


def params(mebibytes):
    return pltpu.CompilerParams(vmem_limit_bytes=mebibytes * 1024 * 1024)


def cost(flops, moved):
    return pl.CostEstimate(flops=flops, bytes_accessed=moved, transcendentals=0)


def shape(dims, kind):
    return jax.ShapeDtypeStruct(dims, kind)


def shards(queries, keys, values, step_rate, memory_init, out_weight):
    axis = "seq"
    size = lax.axis_size(axis)
    place = lax.axis_index(axis).astype(jnp.int32)
    tokens, _ = queries.shape
    local_heads = memory_init.shape[0]
    group_size = math.gcd(local_heads, size, WIN // tokens)
    groups = size // group_size
    heads = local_heads // group_size
    width = heads * BLK
    span = tokens * group_size
    blocks = span // BLK
    reach = WIN // BLK
    members = [[g * group_size + i for i in range(group_size)] for g in range(groups)]
    member = place % group_size
    group = place // group_size
    direct = group_size == 8 and span == WIN and tokens == BLK and groups == 4

    def flip(x, mask):
        return lax.ppermute(x, axis, [(i, i ^ mask) for i in range(size)])

    def onward(x, distance):
        shift = distance * group_size
        return lax.ppermute(x, axis, [(i, i + shift) for i in range(size - shift)])

    last_own = 1 if direct else groups
    where = jnp.stack([member, group, jnp.int32(last_own)])
    dma = pltpu.SemaphoreType.DMA

    if direct:
        *theirs, their_queries = [flip(x, 1) for x in (keys, values, queries)]
        mine = pl.pallas_call(
            pick_kernel,
            out_shape=shape((4, 2, BLK, width), BF16),
            in_specs=[SMEM] + [VMEM] * 2,
            out_specs=VMEM,
            compiler_params=params(4),
            cost_estimate=cost(1, 1),
            name="pick",
        )(where, keys, values)
        sent = pl.pallas_call(
            pair_kernel,
            out_shape=[shape((2, 2, BLK, width), BF16)] * 4,
            in_specs=[SMEM] + [VMEM] * 3,
            out_specs=[VMEM] * 4,
            compiler_params=params(4),
            cost_estimate=cost(1, 1),
            name="pair",
        )(where, mine, *theirs)
        kv = [sent[0]] + [flip(sent[j], 2 * j) for j in range(1, 4)]
        layout = [(j, 0, 2, lambda m, j=j: (m ^ (2 * j)) // 2 * 2) for j in range(4)]
        q_layout = layout
        first = onward(kv[0], 1)
        both = pl.pallas_call(
            join_kernel,
            out_shape=shape((4, 2, BLK, width), BF16),
            in_specs=[VMEM] * 2,
            out_specs=VMEM,
            compiler_params=params(4),
            cost_estimate=cost(2 * 10**9, 1),
            name="join",
        )(*kv[1:3])
        far = [first, onward(both, 1), onward(kv[3], 1)]
        far_layout = [
            layout[0],
            (1, 0, 2, layout[1][3]),
            (1, 2, 2, layout[2][3]),
            (2, 0, 2, layout[3][3]),
        ]
        q = pl.pallas_call(
            pair_queries_kernel,
            out_shape=[shape((2, BLK, width), BF16)] * 4,
            in_specs=[SMEM] + [VMEM] * 2 + [ANY],
            out_specs=[VMEM] * 4,
            compiler_params=params(4),
            cost_estimate=cost(1, 1),
            name="pair_queries",
        )(where, queries, their_queries, first)
        q = [q[0]] + [flip(q[j], 2 * j) for j in range(1, 4)]
    else:

        def by_heads(parts):
            parts = parts.reshape(-1, tokens // BLK, BLK, group_size, width)
            parts = parts.transpose(3, 1, 0, 2, 4)
            if group_size > 1:
                parts = lax.all_to_all(parts, axis, 0, 0, axis_index_groups=members, tiled=True)
            return parts.reshape(blocks, -1, BLK, width)

        kv = [by_heads(jnp.stack([keys, values]))]
        q = [by_heads(queries)[:, 0]]
        far = [onward(kv[0], distance) for distance in range(WIN // span, 0, -1)]
        layout = q_layout = [(0, 0, blocks, lambda m: 0)]
        ready = []
        far_layout = [(c, 0, blocks, lambda m, c=c: c * blocks) for c in range(len(far))]

    total, before, inject = pl.pallas_call(
        functools.partial(memory_kernel, layout),
        out_shape=[
            shape((heads, BLK, 2 * BLK), BF16),
            shape((blocks, heads, BLK, 2 * BLK), BF16),
            shape((blocks, heads, BLK, 2 * BLK), BF16),
        ],
        in_specs=[SMEM, SMEM] + [VMEM] * len(kv),
        out_specs=[VMEM] * 3,
        scratch_shapes=[pltpu.VMEM((blocks, 2, BLK, width), BF16)],
        compiler_params=params(12),
        cost_estimate=cost(1, 1),
        name="memory_updates",
    )(where, lax.dynamic_slice_in_dim(step_rate, member * heads, heads), *kv)

    state_shape = shape((heads, BLK, BLK), F32)
    near, logs, lin, off = pl.pallas_call(
        functools.partial(local_kernel, layout, q_layout),
        out_shape=[
            shape((heads, blocks, BLK, BLK), F32),
            state_shape,
            shape((heads, blocks, BLK, BLK), BF16),
            shape((heads, blocks, BLK, BLK), F32),
        ],
        in_specs=[SMEM] + [VMEM] * (len(kv) + len(q) + 2),
        out_specs=[VMEM] * 4,
        scratch_shapes=[
            pltpu.VMEM((blocks, BLK, width), BF16),
            pltpu.VMEM((blocks, 2, BLK, width), BF16),
        ],
        compiler_params=params(12),
        cost_estimate=cost(1, 1),
        name="attend_own",
    )(where, *kv, *q, before, inject)
    if direct:
        held = flip(total, group_size)
        own, after = pl.pallas_call(
            after_kernel,
            out_shape=[state_shape, shape((heads, BLK, BLK), BF16)],
            in_specs=[SMEM, VMEM, VMEM, HBM, ANY, ANY],
            out_specs=[VMEM, VMEM],
            scratch_shapes=[pltpu.VMEM((heads, BLK, BLK), F32), dma],
            compiler_params=params(8),
            cost_estimate=cost(1, 1),
            name="state_after",
        )(where, held, total, memory_init, logs, far[2])
        moved = flip(after, 2 * group_size)
    else:
        updates = lax.all_gather(
            total, axis, axis_index_groups=[list(x) for x in zip(*members)]
        )
        own = pl.pallas_call(
            chain_kernel,
            out_shape=state_shape,
            in_specs=[SMEM, VMEM, HBM],
            out_specs=VMEM,
            scratch_shapes=[dma],
            compiler_params=params(32),
            name="state_chain",
        )(where, updates, memory_init)
        moved, held = own.astype(BF16), total

    attended = pl.pallas_call(
        functools.partial(far_kernel, far_layout, q_layout),
        out_shape=shape((heads, blocks, BLK, BLK), F32),
        in_specs=[SMEM] + [VMEM] * (2 + len(far) + len(q)),
        out_specs=VMEM,
        scratch_shapes=[
            pltpu.VMEM((blocks, BLK, width), BF16),
            pltpu.VMEM((reach, 2, BLK, width), BF16),
        ],
        compiler_params=params(12),
        cost_estimate=cost(4 * 10**9, 1),
        name="attend_far",
    )(where, near, logs, *far, *q)
    gated = pl.pallas_call(
        gate_kernel,
        out_shape=[shape((tokens, width), BF16)] * group_size,
        in_specs=[SMEM] + [VMEM] * 6,
        out_specs=[VMEM] * group_size,
        compiler_params=params(8),
        cost_estimate=cost(10**9, 1),
        name="gate",
    )(where, attended, lin, off, own, moved, held)
    gated = [gated[0]] + [flip(gated[s], s) for s in range(1, group_size)]
    features = out_weight.shape[1]
    split_out = lax.axis_size("tp") > 1
    projected = []
    middle = group_size // 2
    for start, end in [(0, middle), (middle, group_size)] if middle else [(0, 1)]:
        last = end == group_size
        projected = [
            pl.pallas_call(
                functools.partial(project_kernel, list(range(start, end))),
                out_shape=shape((tokens, features), BF16 if last and not split_out else F32),
                in_specs=[SMEM] + [VMEM] * (1 + end - start + len(projected)),
                out_specs=VMEM,
                compiler_params=params(8),
                cost_estimate=cost(10**9, 1),
                name="project",
            )(where, out_weight, *gated[start:end], *projected)
        ]
    (projected,) = projected
    if split_out:
        projected = lax.psum_scatter(projected, "tp", scatter_dimension=1, tiled=True)
    return projected.astype(BF16)


def solution(mesh):
    return jax.shard_map(
        shards,
        mesh=mesh,
        in_specs=(
            P("seq", "tp"),
            P("seq", "tp"),
            P("seq", "tp"),
            P("tp"),
            P("tp", None, None),
            P("tp", None),
        ),
        out_specs=P("seq", "tp"),
        check_vma=False,
    )
```

```python
import functools
import math

import jax
import jax.numpy as jnp
from jax import lax
from jax.experimental import pallas as pl
from jax.experimental.pallas import tpu as pltpu
from jax.sharding import PartitionSpec as P

WIN = 1024
CH = 16
BLK = 128
MASKED = -1e30
BATCH = 8
SCALE = math.log2(math.e) / math.sqrt(BLK)
F32 = jnp.float32
BF16 = jnp.bfloat16


def dot(a, b):
    return jnp.dot(a.astype(BF16), b.astype(BF16), preferred_element_type=F32)


def dot_nt(a, b):
    return lax.dot_general(a, b, (((1,), (1,)), ((), ())), preferred_element_type=F32)


def dot_tn(a, b):
    return lax.dot_general(a, b, (((0,), (0,)), ((), ())), preferred_element_type=F32)


def earlier_chunk():
    row = lax.broadcasted_iota(jnp.int32, (BLK, BLK), 0) // CH
    col = lax.broadcasted_iota(jnp.int32, (BLK, BLK), 1) // CH
    return row, col, col < row


def at(where_ref, index):
    return where_ref[index]


def head_columns(member, j, width):
    return pl.ds(pl.multiple_of(lax.bitwise_xor(member, 2 * j) * width, width), width)


def pick_kernel(where_ref, k_ref, v_ref, out_ref):
    for j in range(out_ref.shape[0]):
        columns = head_columns(at(where_ref, 0), j, out_ref.shape[-1])
        out_ref[j, 0] = k_ref[:, columns]
        out_ref[j, 1] = v_ref[:, columns]


def pair_kernel(where_ref, mine_ref, k_ref, v_ref, *outs):
    row = at(where_ref, 0) & 1
    for j, out in enumerate(outs):
        columns = head_columns(at(where_ref, 0), j, out.shape[-1])
        out[pl.ds(row, 1)] = mine_ref[j : j + 1]
        out[pl.ds(1 - row, 1), 0] = k_ref[:, columns][None]
        out[pl.ds(1 - row, 1), 1] = v_ref[:, columns][None]


def pair_queries_kernel(where_ref, mine_ref, theirs_ref, _, *outs):
    row = at(where_ref, 0) & 1
    for j, out in enumerate(outs):
        columns = head_columns(at(where_ref, 0), j, out.shape[-1])
        out[pl.ds(row, 1)] = mine_ref[:, columns][None]
        out[pl.ds(1 - row, 1)] = theirs_ref[:, columns][None]


def join_kernel(*refs):
    parts, out_ref = refs[:-2], refs[-1]
    for i, part in enumerate(parts):
        count = part.shape[0]
        out_ref[i * count : (i + 1) * count] = part[...]


def place_pieces(layout, member, pieces, held_ref):
    for piece, index, count, number in layout:
        held_ref[pl.ds(number(member), count)] = pieces[piece][index : index + count]


def wait_all(copies):
    for copy in copies:
        copy.wait()


def memory_kernel(layout, where_ref, rates_ref, *refs):
    pieces, (total_ref, before_ref, inject_ref, kv_ref) = refs[:-4], refs[-4:]
    blocks = before_ref.shape[0]
    heads = total_ref.shape[0]
    place_pieces(layout, at(where_ref, 0), pieces, kv_ref)
    row, col, strict = earlier_chunk()
    near = strict & (row // 2 == col // 2)
    middle = strict & (row // 4 == col // 4) & (row // 2 != col // 2)
    far = strict & (row // 4 != col // 4)
    eye = (
        lax.broadcasted_iota(jnp.int32, (BLK, BLK), 0)
        == lax.broadcasted_iota(jnp.int32, (BLK, BLK), 1)
    ).astype(F32)
    todo = [(b, h) for b in range(blocks) for h in range(heads)]
    every = range(len(todo))
    rate = [rates_ref[at(where_ref, 0) * heads + h] for _, h in todo]
    k, v = [
        [kv_ref[b, t, :, h * BLK : (h + 1) * BLK] for b, h in todo]
        for t in range(2)
    ]
    kf = [x.astype(F32) for x in k]
    norm = [
        lax.rsqrt(BLK * (jnp.mean(x * x, axis=-1, keepdims=True) + 1e-06)) for x in kf
    ]
    unit = [kf[i] * norm[i] for i in every]
    rounded = [x.astype(BF16) for x in unit]
    lower = [dot_nt(rounded[i], rounded[i]) * rate[i] for i in every]
    half = [-jnp.where(near, x, 0.0) for x in lower]
    for region in (middle, far):
        inv = [(x + eye).astype(BF16) for x in half]
        part = [dot(jnp.where(region, lower[i], 0.0), inv[i]) for i in every]
        half = [half[i] - dot(inv[i], part[i]) for i in every]
    both = [dot(half[i], jnp.concatenate([rounded[i], v[i]], axis=1)) for i in every]
    both = [
        both[i] + jnp.concatenate([unit[i], v[i].astype(F32)], axis=1) for i in every
    ]
    weighted = [(both[i] * (norm[i] * rate[i])).astype(BF16) for i in every]
    for i, (b, h) in enumerate(todo):
        inject_ref[b, h] = weighted[i]
    change = [dot_tn(k[i], weighted[i]) for i in every]
    running = [jnp.concatenate([eye, jnp.zeros_like(eye)], axis=1) for _ in range(heads)]
    for i, (b, h) in enumerate(todo):
        before = running[h].astype(BF16)
        before_ref[b, h] = before
        after = running[h] - dot(change[i][:, :BLK], before)
        running[h] = jnp.concatenate(
            [after[:, :BLK], after[:, BLK:] + change[i][:, BLK:]], axis=1
        )
    for h in range(heads):
        total_ref[h] = running[h].astype(BF16)


def own_state(where_ref, init_hbm, init_ref, sem):
    heads = init_ref.shape[0]
    copy = pltpu.make_async_copy(init_hbm.at[pl.ds(at(where_ref, 0) * heads, heads)], init_ref, sem)
    copy.start()
    return copy


def advance(update, state):
    return dot(update[:, :BLK], state) + update[:, BLK:].astype(F32)


def after_kernel(where_ref, held_ref, total_ref, init_hbm, *refs):
    own_ref, after_ref, init_ref, sem = refs[-4:]
    own_state(where_ref, init_hbm, init_ref, sem).wait()
    second = at(where_ref, 1) % 2 == 1
    for h in range(after_ref.shape[0]):
        state = init_ref[h]
        earlier = advance(jnp.where(second, held_ref[h], total_ref[h]), state)
        own_ref[h] = jnp.where(second, earlier, state)
        later = jnp.where(second, total_ref[h], held_ref[h])
        after_ref[h] = advance(later, earlier).astype(BF16)


def chain_kernel(where_ref, updates_ref, init_hbm, state_ref, sem):
    own_state(where_ref, init_hbm, state_ref, sem).wait()

    @pl.loop(0, at(where_ref, 1))
    def _(g):
        for h in range(state_ref.shape[0]):
            state_ref[h] = advance(updates_ref[g, h], state_ref[h])


def within_block():
    row = lax.broadcasted_iota(jnp.int32, (BLK, BLK), 0)
    col = lax.broadcasted_iota(jnp.int32, (BLK, BLK), 1)
    return row, col


def weigh(p, v):
    return jnp.dot(p, jnp.concatenate([v, jnp.ones_like(v)], axis=1), preferred_element_type=F32)


def batches(blocks, heads):
    todo = [(b, h) for b in range(blocks) for h in range(heads)]
    return [todo[i : i + BATCH] for i in range(0, len(todo), BATCH)]


def local_kernel(kv_layout, q_layout, where_ref, *refs):
    kv_pieces = refs[: len(kv_layout)]
    q_pieces = refs[len(kv_layout) : len(kv_layout) + len(q_layout)]
    before_ref, inject_ref = refs[len(kv_layout) + len(q_layout) :][:2]
    attended_ref, logs_ref, lin_ref, off_ref, q_ref, kv_ref = refs[-6:]
    blocks = kv_ref.shape[0]
    heads = attended_ref.shape[0]
    place_pieces(q_layout, at(where_ref, 0), q_pieces, q_ref)
    place_pieces(kv_layout, at(where_ref, 0), kv_pieces, kv_ref)
    row, col = within_block()
    logs = [jnp.zeros((BLK, BLK), F32) for _ in range(heads)]
    for part in batches(blocks, heads):
        scores = []
        for b, h in part:
            columns = slice(h * BLK, (h + 1) * BLK)
            q = q_ref[b, :, columns]
            s = jnp.where(col <= row, dot_nt(q, kv_ref[b, 0, :, columns]), MASKED)
            if b > 0:
                k = kv_ref[0:b, 0, :, columns].reshape(b * BLK, BLK)
                s = jnp.concatenate([dot_nt(q, k), s], axis=1)
            scores.append(s)
        top = [jnp.max(s, axis=-1, keepdims=True) * SCALE for s in scores]
        p = [jnp.exp2(s * SCALE - t).astype(BF16) for s, t in zip(scores, top)]
        for i, (b, h) in enumerate(part):
            columns = slice(h * BLK, (h + 1) * BLK)
            v = kv_ref[0 : b + 1, 1, :, columns].reshape((b + 1) * BLK, BLK)
            acc = weigh(p[i], v)
            total = acc[:, BLK:]
            attended_ref[h, b] = acc[:, :BLK] / total
            logs[h] = jnp.where(col == b, jnp.log2(total) + top[i], logs[h])
    for h in range(heads):
        logs_ref[h] = logs[h]
    strict = earlier_chunk()[2]
    todo = [(b, h) for b in range(blocks) for h in range(heads)]
    every = range(len(todo))
    q = [q_ref[b, :, h * BLK : (h + 1) * BLK] for b, h in todo]
    inner = [
        jnp.where(strict, dot_nt(q[i], kv_ref[b, 0, :, h * BLK : (h + 1) * BLK]), 0.0)
        for i, (b, h) in enumerate(todo)
    ]
    inside = [dot(inner[i], inject_ref[b, h]) for i, (b, h) in enumerate(todo)]
    rows = [
        dot(q[i].astype(F32) - inside[i][:, :BLK], before_ref[b, h])
        for i, (b, h) in enumerate(todo)
    ]
    for i, (b, h) in enumerate(todo):
        lin_ref[h, b] = rows[i][:, :BLK].astype(BF16)
        off_ref[h, b] = rows[i][:, BLK:] + inside[i][:, BLK:]


def far_kernel(layout, q_layout, where_ref, near_ref, logs_ref, *refs):
    pieces, q_pieces = refs[: -3 - len(q_layout)], refs[-3 - len(q_layout) : -3]
    out_ref, q_ref, kv_ref = refs[-3:]
    reach = kv_ref.shape[0]
    blocks = q_ref.shape[0]
    place_pieces(q_layout, at(where_ref, 0), q_pieces, q_ref)
    place_pieces(layout, at(where_ref, 0), pieces, kv_ref)
    row, col = within_block()
    hidden = [
        jnp.where(at(where_ref, 1) * blocks + c < reach, MASKED, 0.0) for c in range(reach)
    ]
    for part in batches(blocks, near_ref.shape[0]):
        scores = []
        for b, h in part:
            columns = slice(h * BLK, (h + 1) * BLK)
            k = kv_ref[b:reach, 0, :, columns].reshape((reach - b) * BLK, BLK)
            s = dot_nt(q_ref[b, :, columns], k)
            s = [s[:, i * BLK : (i + 1) * BLK] + hidden[b + i] for i in range(reach - b)]
            s[0] = jnp.where(col > row, s[0], MASKED)
            scores.append(jnp.concatenate(s, axis=1) if len(s) > 1 else s[0])
        old = [logs_ref[h][:, b : b + 1] for b, h in part]
        top = [
            jnp.maximum(jnp.max(s, axis=-1, keepdims=True) * SCALE, t)
            for s, t in zip(scores, old)
        ]
        p = [jnp.exp2(s * SCALE - t).astype(BF16) for s, t in zip(scores, top)]
        kept = [jnp.exp2(o - t) for o, t in zip(old, top)]
        for i, (b, h) in enumerate(part):
            columns = slice(h * BLK, (h + 1) * BLK)
            v = kv_ref[b:reach, 1, :, columns].reshape((reach - b) * BLK, BLK)
            acc = weigh(p[i], v)
            sums = acc[:, :BLK] + near_ref[h, b] * kept[i]
            out_ref[h, b] = sums / (acc[:, BLK:] + kept[i])


def gate_kernel(where_ref, attended_ref, lin_ref, off_ref, own_ref, moved_ref, held_ref, *refs):
    outs = refs
    heads, blocks = lin_ref.shape[:2]
    count = blocks // len(outs)
    late = at(where_ref, 1) > at(where_ref, 2)
    odd = at(where_ref, 1) % 2 == 1
    state = []
    for h in range(heads):
        moved = moved_ref[h].astype(F32)
        moved = jnp.where(odd, advance(held_ref[h], moved), moved)
        state.append(jnp.where(late, moved, own_ref[h]).astype(BF16))
    numbers = [lax.bitwise_xor(at(where_ref, 0), s) * count for s in range(len(outs))]
    todo = [(s, i, h) for s in range(len(outs)) for i in range(count) for h in range(heads)]
    read = [
        dot(lin_ref[h, numbers[s] + i], state[h]) + off_ref[h, numbers[s] + i]
        for s, i, h in todo
    ]
    for (s, i, h), r in zip(todo, read):
        gated = attended_ref[h, numbers[s] + i] * jax.nn.sigmoid(r)
        rows = slice(i * BLK, (i + 1) * BLK)
        outs[s][rows, h * BLK : (h + 1) * BLK] = gated.astype(BF16)


def project_kernel(place, where_ref, w_ref, *refs):
    pieces, before = refs[: len(place)], refs[len(place) : -3]
    out_ref, held_ref, sem = refs[-3:]
    width = pieces[0].shape[1]
    rows = [
        pl.ds(pl.multiple_of(lax.bitwise_xor(at(where_ref, 0), s) * width, width), width)
        for s in place
    ]
    tile = math.gcd(out_ref.shape[1], 512)
    stores = []
    for start in range(0, out_ref.shape[1], tile):
        columns = pl.ds(start, tile)
        acc = before[0][:, columns] if before else jnp.zeros((out_ref.shape[0], tile), F32)
        for row, piece in zip(rows, pieces):
            acc += jnp.dot(piece[...], w_ref[row, columns], preferred_element_type=F32)
        held_ref[:, columns] = acc.astype(out_ref.dtype)
        stores.append(
            pltpu.make_async_copy(held_ref.at[:, columns], out_ref.at[:, columns], sem)
        )
        stores[-1].start()
    wait_all(stores)


def partial_kernel(place, where_ref, w_ref, *refs):
    pieces, out_ref = refs[:-1], refs[-1]
    width = pieces[0].shape[1]
    acc = jnp.zeros(out_ref.shape, F32)
    for s, piece in zip(place, pieces):
        first = pl.multiple_of(lax.bitwise_xor(at(where_ref, 0), s) * width, width)
        acc += jnp.dot(piece[...], w_ref[pl.ds(first, width), :], preferred_element_type=F32)
    out_ref[...] = acc


VMEM = pl.BlockSpec(memory_space=pltpu.VMEM)
ANY = pl.BlockSpec(memory_space=pl.ANY)
HBM = pl.BlockSpec(memory_space=pltpu.HBM)
SMEM = pl.BlockSpec(memory_space=pltpu.SMEM)


def params(mebibytes):
    return pltpu.CompilerParams(vmem_limit_bytes=mebibytes * 1024 * 1024)


def cost(flops, moved):
    return pl.CostEstimate(flops=flops, bytes_accessed=moved, transcendentals=0)


def shape(dims, kind):
    return jax.ShapeDtypeStruct(dims, kind)


def shards(queries, keys, values, step_rate, memory_init, out_weight):
    axis = "seq"
    size = lax.axis_size(axis)
    place = lax.axis_index(axis).astype(jnp.int32)
    tokens, _ = queries.shape
    local_heads = memory_init.shape[0]
    group_size = math.gcd(local_heads, size, WIN // tokens)
    groups = size // group_size
    heads = local_heads // group_size
    width = heads * BLK
    span = tokens * group_size
    blocks = span // BLK
    reach = WIN // BLK
    members = [[g * group_size + i for i in range(group_size)] for g in range(groups)]
    member = place % group_size
    group = place // group_size
    direct = group_size == 8 and span == WIN and tokens == BLK and groups == 4

    def flip(x, mask):
        return lax.ppermute(x, axis, [(i, i ^ mask) for i in range(size)])

    def onward(x, distance):
        shift = distance * group_size
        return lax.ppermute(x, axis, [(i, i + shift) for i in range(size - shift)])

    last_own = 1 if direct else groups
    where = jnp.stack([member, group, jnp.int32(last_own)])
    dma = pltpu.SemaphoreType.DMA
    state_shape = shape((heads, BLK, BLK), F32)

    def hold(parts, after):
        return pl.pallas_call(
            join_kernel,
            out_shape=shape((2 * len(parts), 2, BLK, width), BF16),
            in_specs=[VMEM] * len(parts) + [ANY],
            out_specs=VMEM,
            compiler_params=params(4),
            cost_estimate=cost(1, 1),
            name="join",
        )(*parts, after)

    if direct:
        *theirs, their_queries = [flip(x, 1) for x in (keys, values, queries)]
        mine = pl.pallas_call(
            pick_kernel,
            out_shape=shape((4, 2, BLK, width), BF16),
            in_specs=[SMEM] + [VMEM] * 2,
            out_specs=VMEM,
            compiler_params=params(4),
            cost_estimate=cost(1, 1),
            name="pick",
        )(where, keys, values)
        sent = pl.pallas_call(
            pair_kernel,
            out_shape=[shape((2, 2, BLK, width), BF16)] * 4,
            in_specs=[SMEM] + [VMEM] * 3,
            out_specs=[VMEM] * 4,
            compiler_params=params(4),
            cost_estimate=cost(3*10**9, 1),
            name="pair",
        )(where, mine, *theirs)
        kv = [sent[0]] + [flip(sent[j], 2 * j) for j in range(1, 4)]
        layout = [(j, 0, 2, lambda m, j=j: (m ^ (2 * j)) // 2 * 2) for j in range(4)]
        q_layout = layout
        first = onward(kv[0], 1)
        second = onward(kv[1], 1)
        q = pl.pallas_call(
            pair_queries_kernel,
            out_shape=[shape((2, BLK, width), BF16)] * 4,
            in_specs=[SMEM] + [VMEM] * 2 + [ANY],
            out_specs=[VMEM] * 4,
            compiler_params=params(4),
            cost_estimate=cost(1, 1),
            name="pair_queries",
        )(where, queries, their_queries, kv[1])
        far = [first, second, onward(kv[2], 1)]
        far_layout = layout
        earlier = [second, first]
        ready = []
        q = [q[0]] + [flip(q[j], 2 * j) for j in range(1, 4)]
    else:
        earlier = []
        ready = []
        def by_heads(parts):
            parts = parts.reshape(-1, tokens // BLK, BLK, group_size, width)
            parts = parts.transpose(3, 1, 0, 2, 4)
            if group_size > 1:
                parts = lax.all_to_all(parts, axis, 0, 0, axis_index_groups=members, tiled=True)
            return parts.reshape(blocks, -1, BLK, width)

        kv = [by_heads(jnp.stack([keys, values]))]
        q = [by_heads(queries)[:, 0]]
        far = [onward(kv[0], distance) for distance in range(WIN // span, 0, -1)]
        layout = q_layout = [(0, 0, blocks, lambda m: 0)]
        ready = []
        far_layout = [(c, 0, blocks, lambda m, c=c: c * blocks) for c in range(len(far))]

    total, before, inject = pl.pallas_call(
        functools.partial(memory_kernel, layout),
        out_shape=[
            shape((heads, BLK, 2 * BLK), BF16),
            shape((blocks, heads, BLK, 2 * BLK), BF16),
            shape((blocks, heads, BLK, 2 * BLK), BF16),
        ],
        in_specs=[SMEM] * 2 + [VMEM] * len(kv) + [ANY] * len(earlier),
        out_specs=[VMEM] * 3,
        scratch_shapes=[pltpu.VMEM((blocks, 2, BLK, width), BF16)],
        compiler_params=params(12),
        cost_estimate=cost(50 * 10**8, 1),
        name="memory_updates",
    )(where, step_rate, *kv, *earlier)

    near, logs, lin, off = pl.pallas_call(
        functools.partial(local_kernel, layout, q_layout),
        out_shape=[
            shape((heads, blocks, BLK, BLK), F32),
            state_shape,
            shape((heads, blocks, BLK, BLK), BF16),
            shape((heads, blocks, BLK, BLK), F32),
        ],
        in_specs=[SMEM] + [VMEM] * (len(kv) + len(q) + 2) + [ANY] * len(ready),
        out_specs=[VMEM] * 4,
        scratch_shapes=[
            pltpu.VMEM((blocks, BLK, width), BF16),
            pltpu.VMEM((blocks, 2, BLK, width), BF16),
        ],
        compiler_params=params(12),
        cost_estimate=cost(40 * 10**8, 1),
        name="attend_own",
    )(where, *kv, *q, before, inject, *ready)
    if direct:
        held = flip(total, group_size)
        far.append(onward(hold(kv[3:], total), 1))
        own, after = pl.pallas_call(
            after_kernel,
            out_shape=[state_shape, shape((heads, BLK, BLK), BF16)],
            in_specs=[SMEM] + [VMEM] * 2 + [HBM, ANY],
            out_specs=[VMEM, VMEM],
            scratch_shapes=[pltpu.VMEM((heads, BLK, BLK), F32), dma],
            compiler_params=params(8),
            cost_estimate=cost(1, 1),
            name="state_after",
        )(where, held, total, memory_init, far[2])
        moved = flip(after, 2 * group_size)
    else:
        updates = lax.all_gather(
            total, axis, axis_index_groups=[list(x) for x in zip(*members)]
        )
        own = pl.pallas_call(
            chain_kernel,
            out_shape=state_shape,
            in_specs=[SMEM, VMEM, HBM],
            out_specs=VMEM,
            scratch_shapes=[dma],
            compiler_params=params(32),
            name="state_chain",
        )(where, updates, memory_init)
        moved, held = own.astype(BF16), total

    attended = pl.pallas_call(
        functools.partial(far_kernel, far_layout, q_layout),
        out_shape=shape((heads, blocks, BLK, BLK), F32),
        in_specs=[SMEM] + [VMEM] * (2 + len(far) + len(q)),
        out_specs=VMEM,
        scratch_shapes=[
            pltpu.VMEM((blocks, BLK, width), BF16),
            pltpu.VMEM((reach, 2, BLK, width), BF16),
        ],
        compiler_params=params(12),
        cost_estimate=cost(4 * 10**9, 1),
        name="attend_far",
    )(where, near, logs, *far, *q)
    gated = pl.pallas_call(
        gate_kernel,
        out_shape=[shape((tokens, width), BF16)] * group_size,
        in_specs=[SMEM] + [VMEM] * 6,
        out_specs=[VMEM] * group_size,
        compiler_params=params(8),
        cost_estimate=cost(10**9, 1),
        name="gate",
    )(where, attended, lin, off, own, moved, held)
    gated = [gated[0]] + [flip(gated[s], s) for s in range(1, group_size)]
    features = out_weight.shape[1]
    split_out = lax.axis_size("tp") > 1
    part = []
    early = list(range(6 if group_size == 8 else 0))
    if early:
        part = [
            pl.pallas_call(
                functools.partial(partial_kernel, early),
                out_shape=shape((tokens, features), F32),
                in_specs=[SMEM] + [VMEM] * (1 + len(early)),
                out_specs=VMEM,
                compiler_params=params(8),
                cost_estimate=cost(10**9, 1),
                name="project_early",
            )(where, out_weight, *[gated[s] for s in early])
        ]
    late = list(range(len(early), group_size))
    kind = F32 if split_out else BF16
    projected = pl.pallas_call(
        functools.partial(project_kernel, late),
        out_shape=shape((tokens, features), kind),
        in_specs=[SMEM] + [VMEM] * (1 + len(late) + len(part)),
        out_specs=HBM,
        scratch_shapes=[pltpu.VMEM((tokens, features), kind), dma],
        compiler_params=params(8),
        cost_estimate=cost(10**9, 1),
        name="project",
    )(where, out_weight, *[gated[s] for s in late], *part)
    if split_out:
        projected = lax.psum_scatter(projected, "tp", scatter_dimension=1, tiled=True)
    return projected.astype(BF16)


def solution(mesh):
    return jax.shard_map(
        shards,
        mesh=mesh,
        in_specs=(
            P("seq", "tp"),
            P("seq", "tp"),
            P("seq", "tp"),
            P("tp"),
            P("tp", None, None),
            P("tp", None),
        ),
        out_specs=P("seq", "tp"),
        check_vma=False,
    )
```

```python
import functools
import math

import jax
import jax.numpy as jnp
from jax import lax
from jax.experimental import pallas as pl
from jax.experimental.pallas import tpu as pltpu
from jax.sharding import PartitionSpec as P

WIN = 1024
CH = 16
BLK = 128
MASKED = -1e30
SCALE = math.log2(math.e) / math.sqrt(BLK)
F32 = jnp.float32
BF16 = jnp.bfloat16


def dot(a, b):
    return jnp.dot(a.astype(BF16), b.astype(BF16), preferred_element_type=F32)


def dot_nt(a, b):
    return lax.dot_general(a, b, (((1,), (1,)), ((), ())), preferred_element_type=F32)


def dot_tn(a, b):
    return lax.dot_general(a, b, (((0,), (0,)), ((), ())), preferred_element_type=F32)


def earlier_chunk():
    row = lax.broadcasted_iota(jnp.int32, (BLK, BLK), 0) // CH
    col = lax.broadcasted_iota(jnp.int32, (BLK, BLK), 1) // CH
    return row, col, col < row


def at(where_ref, index):
    return where_ref[index]


def head_columns(member, j, width):
    return pl.ds(pl.multiple_of(lax.bitwise_xor(member, 2 * j) * width, width), width)


def pick_kernel(where_ref, k_ref, v_ref, out_ref, sem):
    copies = []
    for j in range(out_ref.shape[0]):
        columns = head_columns(at(where_ref, 0), j, out_ref.shape[-1])
        for t, source in enumerate((k_ref, v_ref)):
            copies.append(pltpu.make_async_copy(source.at[:, columns], out_ref.at[j, t], sem))
            copies[-1].start()
    wait_all(copies)


def pair_kernel(where_ref, mine_ref, k_ref, v_ref, *outs):
    row = at(where_ref, 0) & 1
    for j, out in enumerate(outs):
        columns = head_columns(at(where_ref, 0), j, out.shape[-1])
        out[pl.ds(row, 1)] = mine_ref[j : j + 1]
        out[pl.ds(1 - row, 1), 0] = k_ref[:, columns][None]
        out[pl.ds(1 - row, 1), 1] = v_ref[:, columns][None]


def pair_queries_kernel(where_ref, mine_ref, theirs_ref, _, *outs):
    row = at(where_ref, 0) & 1
    for j, out in enumerate(outs):
        columns = head_columns(at(where_ref, 0), j, out.shape[-1])
        out[pl.ds(row, 1)] = mine_ref[:, columns][None]
        out[pl.ds(1 - row, 1)] = theirs_ref[:, columns][None]


def join_kernel(*refs):
    parts, out_ref = refs[:-2], refs[-1]
    for i, part in enumerate(parts):
        count = part.shape[0]
        out_ref[i * count : (i + 1) * count] = part[...]


def place_pieces(layout, member, pieces, held_ref):
    for piece, index, count, number in layout:
        held_ref[pl.ds(number(member), count)] = pieces[piece][index : index + count]


def wait_all(copies):
    for copy in copies:
        copy.wait()


def memory_kernel(layout, where_ref, rates_ref, *refs):
    pieces, (total_ref, before_ref, inject_ref, kv_ref) = refs[:-4], refs[-4:]
    blocks = before_ref.shape[0]
    heads = total_ref.shape[0]
    place_pieces(layout, at(where_ref, 0), pieces, kv_ref)
    row, col, strict = earlier_chunk()
    near = strict & (row // 2 == col // 2)
    middle = strict & (row // 4 == col // 4) & (row // 2 != col // 2)
    far = strict & (row // 4 != col // 4)
    eye = (
        lax.broadcasted_iota(jnp.int32, (BLK, BLK), 0)
        == lax.broadcasted_iota(jnp.int32, (BLK, BLK), 1)
    ).astype(F32)
    todo = [(b, h) for b in range(blocks) for h in range(heads)]
    every = range(len(todo))
    rate = [rates_ref[at(where_ref, 0) * heads + h] for _, h in todo]
    k, v = [
        [kv_ref[b, t, :, h * BLK : (h + 1) * BLK] for b, h in todo]
        for t in range(2)
    ]
    kf = [x.astype(F32) for x in k]
    norm = [
        lax.rsqrt(BLK * (jnp.mean(x * x, axis=-1, keepdims=True) + 1e-06)) for x in kf
    ]
    unit = [kf[i] * norm[i] for i in every]
    rounded = [x.astype(BF16) for x in unit]
    lower = [dot_nt(rounded[i], rounded[i]) * rate[i] for i in every]
    half = [-jnp.where(near, x, 0.0) for x in lower]
    for region in (middle, far):
        inv = [(x + eye).astype(BF16) for x in half]
        part = [dot(jnp.where(region, lower[i], 0.0), inv[i]) for i in every]
        half = [half[i] - dot(inv[i], part[i]) for i in every]
    both = [dot(half[i], jnp.concatenate([rounded[i], v[i]], axis=1)) for i in every]
    both = [
        both[i] + jnp.concatenate([unit[i], v[i].astype(F32)], axis=1) for i in every
    ]
    weighted = [(both[i] * (norm[i] * rate[i])).astype(BF16) for i in every]
    for i, (b, h) in enumerate(todo):
        inject_ref[b, h] = weighted[i]
    change = [dot_tn(k[i], weighted[i]) for i in every]
    running = [jnp.concatenate([eye, jnp.zeros_like(eye)], axis=1) for _ in range(heads)]
    for i, (b, h) in enumerate(todo):
        before = running[h].astype(BF16)
        before_ref[b, h] = before
        after = running[h] - dot(change[i][:, :BLK], before)
        running[h] = jnp.concatenate(
            [after[:, :BLK], after[:, BLK:] + change[i][:, BLK:]], axis=1
        )
    for h in range(heads):
        total_ref[h] = running[h].astype(BF16)


def own_state(where_ref, init_hbm, init_ref, sem):
    heads = init_ref.shape[0]
    copy = pltpu.make_async_copy(init_hbm.at[pl.ds(at(where_ref, 0) * heads, heads)], init_ref, sem)
    copy.start()
    return copy


def advance(update, state):
    return dot(update[:, :BLK], state) + update[:, BLK:].astype(F32)


def after_kernel(where_ref, held_ref, total_ref, init_ref, *refs):
    own_ref, after_ref = refs[-2:]
    heads = own_ref.shape[0]
    second = at(where_ref, 1) % 2 == 1
    for h in range(after_ref.shape[0]):
        state = init_ref[at(where_ref, 0) * heads + h]
        earlier = advance(jnp.where(second, held_ref[h], total_ref[h]), state)
        own_ref[h] = jnp.where(second, earlier, state)
        later = jnp.where(second, total_ref[h], held_ref[h])
        after_ref[h] = advance(later, earlier).astype(BF16)


def chain_kernel(where_ref, updates_ref, init_hbm, state_ref, sem):
    own_state(where_ref, init_hbm, state_ref, sem).wait()

    @pl.loop(0, at(where_ref, 1))
    def _(g):
        for h in range(state_ref.shape[0]):
            state_ref[h] = advance(updates_ref[g, h], state_ref[h])


def within_block():
    row = lax.broadcasted_iota(jnp.int32, (BLK, BLK), 0)
    col = lax.broadcasted_iota(jnp.int32, (BLK, BLK), 1)
    return row, col


def weigh(p, v):
    return jnp.dot(p, jnp.concatenate([v, jnp.ones_like(v)], axis=1), preferred_element_type=F32)


def batches(blocks, heads, count):
    todo = [(b, h) for b in range(blocks) for h in range(heads)]
    return [todo[i : i + count] for i in range(0, len(todo), count)]


def local_kernel(kv_layout, q_layout, where_ref, *refs):
    kv_pieces = refs[: len(kv_layout)]
    q_pieces = refs[len(kv_layout) : len(kv_layout) + len(q_layout)]
    before_ref, inject_ref = refs[len(kv_layout) + len(q_layout) :][:2]
    attended_ref, logs_ref, lin_ref, off_ref, q_ref, kv_ref = refs[-6:]
    blocks = kv_ref.shape[0]
    heads = attended_ref.shape[0]
    place_pieces(q_layout, at(where_ref, 0), q_pieces, q_ref)
    place_pieces(kv_layout, at(where_ref, 0), kv_pieces, kv_ref)
    row, col = within_block()
    logs = [jnp.zeros((BLK, BLK), F32) for _ in range(heads)]
    for part in batches(blocks, heads, 16):
        scores = []
        for b, h in part:
            columns = slice(h * BLK, (h + 1) * BLK)
            q = q_ref[b, :, columns]
            s = jnp.where(col <= row, dot_nt(q, kv_ref[b, 0, :, columns]), MASKED)
            if b > 0:
                k = kv_ref[0:b, 0, :, columns].reshape(b * BLK, BLK)
                s = jnp.concatenate([dot_nt(q, k), s], axis=1)
            scores.append(s)
        top = [jnp.max(s, axis=-1, keepdims=True) * SCALE for s in scores]
        p = [jnp.exp2(s * SCALE - t).astype(BF16) for s, t in zip(scores, top)]
        for i, (b, h) in enumerate(part):
            columns = slice(h * BLK, (h + 1) * BLK)
            v = kv_ref[0 : b + 1, 1, :, columns].reshape((b + 1) * BLK, BLK)
            acc = weigh(p[i], v)
            total = acc[:, BLK:]
            attended_ref[h, b] = acc[:, :BLK] / total
            logs[h] = jnp.where(col == b, jnp.log2(total) + top[i], logs[h])
    for h in range(heads):
        logs_ref[h] = logs[h]
    strict = earlier_chunk()[2]
    todo = [(b, h) for b in range(blocks) for h in range(heads)]
    every = range(len(todo))
    q = [q_ref[b, :, h * BLK : (h + 1) * BLK] for b, h in todo]
    inner = [
        jnp.where(strict, dot_nt(q[i], kv_ref[b, 0, :, h * BLK : (h + 1) * BLK]), 0.0)
        for i, (b, h) in enumerate(todo)
    ]
    inside = [dot(inner[i], inject_ref[b, h]) for i, (b, h) in enumerate(todo)]
    rows = [
        dot(q[i].astype(F32) - inside[i][:, :BLK], before_ref[b, h])
        for i, (b, h) in enumerate(todo)
    ]
    for i, (b, h) in enumerate(todo):
        lin_ref[h, b] = rows[i][:, :BLK].astype(BF16)
        off_ref[h, b] = rows[i][:, BLK:] + inside[i][:, BLK:]


def far_kernel(layout, q_layout, where_ref, near_ref, logs_ref, *refs):
    pieces, q_pieces = refs[: -3 - len(q_layout)], refs[-3 - len(q_layout) : -3]
    out_ref, q_ref, kv_ref = refs[-3:]
    reach = kv_ref.shape[0]
    blocks = q_ref.shape[0]
    place_pieces(q_layout, at(where_ref, 0), q_pieces, q_ref)
    place_pieces(layout, at(where_ref, 0), pieces, kv_ref)
    row, col = within_block()
    whole = blocks == reach
    hidden = [
        jnp.where(at(where_ref, 1) * blocks + c < reach, MASKED, 0.0) for c in range(reach)
    ]
    for part in batches(blocks, near_ref.shape[0], 4):
        scores = []
        for b, h in part:
            columns = slice(h * BLK, (h + 1) * BLK)
            k = kv_ref[b:reach, 0, :, columns].reshape((reach - b) * BLK, BLK)
            s = dot_nt(q_ref[b, :, columns], k)
            s = [s[:, i * BLK : (i + 1) * BLK] for i in range(reach - b)]
            if not whole:
                s = [x + hidden[b + i] for i, x in enumerate(s)]
            s[0] = jnp.where(col > row, s[0], MASKED)
            scores.append(jnp.concatenate(s, axis=1) if len(s) > 1 else s[0])
        old = [logs_ref[h][:, b : b + 1] for b, h in part]
        top = [
            jnp.maximum(jnp.max(s, axis=-1, keepdims=True) * SCALE, t)
            for s, t in zip(scores, old)
        ]
        p = [jnp.exp2(s * SCALE - t).astype(BF16) for s, t in zip(scores, top)]
        kept = [jnp.exp2(o - t) for o, t in zip(old, top)]
        for i, (b, h) in enumerate(part):
            columns = slice(h * BLK, (h + 1) * BLK)
            v = kv_ref[b:reach, 1, :, columns].reshape((reach - b) * BLK, BLK)
            acc = weigh(p[i], v)
            sums = acc[:, :BLK] + near_ref[h, b] * kept[i]
            sums = sums / (acc[:, BLK:] + kept[i])
            if whole:
                sums = jnp.where(at(where_ref, 1) == 0, near_ref[h, b], sums)
            out_ref[h, b] = sums


def gate_kernel(where_ref, attended_ref, lin_ref, off_ref, own_ref, moved_ref, held_ref, *refs):
    outs = refs
    heads, blocks = lin_ref.shape[:2]
    count = blocks // len(outs)
    late = at(where_ref, 1) > at(where_ref, 2)
    odd = at(where_ref, 1) % 2 == 1
    state = []
    for h in range(heads):
        moved = moved_ref[h].astype(F32)
        moved = jnp.where(odd, advance(held_ref[h], moved), moved)
        state.append(jnp.where(late, moved, own_ref[h]).astype(BF16))
    numbers = [lax.bitwise_xor(at(where_ref, 0), s) * count for s in range(len(outs))]
    todo = [(s, i, h) for s in range(len(outs)) for i in range(count) for h in range(heads)]
    read = [
        dot(lin_ref[h, numbers[s] + i], state[h]) + off_ref[h, numbers[s] + i]
        for s, i, h in todo
    ]
    for (s, i, h), r in zip(todo, read):
        gated = attended_ref[h, numbers[s] + i] * jax.nn.sigmoid(r)
        rows = slice(i * BLK, (i + 1) * BLK)
        outs[s][rows, h * BLK : (h + 1) * BLK] = gated.astype(BF16)


def project_kernel(place, where_ref, w_ref, *refs):
    pieces, before = refs[: len(place)], refs[len(place) : -3]
    out_ref, held_ref, sem = refs[-3:]
    width = pieces[0].shape[1]
    rows = [
        pl.ds(pl.multiple_of(lax.bitwise_xor(at(where_ref, 0), s) * width, width), width)
        for s in place
    ]
    tile = math.gcd(out_ref.shape[1], 256)
    stores = []
    for start in range(0, out_ref.shape[1], tile):
        columns = pl.ds(start, tile)
        acc = before[0][:, columns] if before else jnp.zeros((out_ref.shape[0], tile), F32)
        for row, piece in zip(rows, pieces):
            acc += jnp.dot(piece[...], w_ref[row, columns], preferred_element_type=F32)
        held_ref[:, columns] = acc.astype(out_ref.dtype)
        stores.append(
            pltpu.make_async_copy(held_ref.at[:, columns], out_ref.at[:, columns], sem)
        )
        stores[-1].start()
    wait_all(stores)


def partial_kernel(place, where_ref, w_ref, *refs):
    pieces, out_ref = refs[:-1], refs[-1]
    width = pieces[0].shape[1]
    acc = jnp.zeros(out_ref.shape, F32)
    for s, piece in zip(place, pieces):
        first = pl.multiple_of(lax.bitwise_xor(at(where_ref, 0), s) * width, width)
        acc += jnp.dot(piece[...], w_ref[pl.ds(first, width), :], preferred_element_type=F32)
    out_ref[...] = acc


VMEM = pl.BlockSpec(memory_space=pltpu.VMEM)
ANY = pl.BlockSpec(memory_space=pl.ANY)
HBM = pl.BlockSpec(memory_space=pltpu.HBM)
SMEM = pl.BlockSpec(memory_space=pltpu.SMEM)


def params(mebibytes):
    return pltpu.CompilerParams(vmem_limit_bytes=mebibytes * 1024 * 1024)


def cost(flops, moved):
    return pl.CostEstimate(flops=flops, bytes_accessed=moved, transcendentals=0)


def shape(dims, kind):
    return jax.ShapeDtypeStruct(dims, kind)


def shards(queries, keys, values, step_rate, memory_init, out_weight):
    axis = "seq"
    size = lax.axis_size(axis)
    place = lax.axis_index(axis).astype(jnp.int32)
    tokens, _ = queries.shape
    local_heads = memory_init.shape[0]
    group_size = math.gcd(local_heads, size, WIN // tokens)
    groups = size // group_size
    heads = local_heads // group_size
    width = heads * BLK
    span = tokens * group_size
    blocks = span // BLK
    reach = WIN // BLK
    members = [[g * group_size + i for i in range(group_size)] for g in range(groups)]
    member = place % group_size
    group = place // group_size
    direct = group_size == 8 and span == WIN and tokens == BLK and groups == 4

    def flip(x, mask):
        return lax.ppermute(x, axis, [(i, i ^ mask) for i in range(size)])

    def onward(x, distance):
        shift = distance * group_size
        return lax.ppermute(x, axis, [(i, i + shift) for i in range(size - shift)])

    last_own = 1 if direct else groups
    where = jnp.stack([member, group, jnp.int32(last_own)])
    dma = pltpu.SemaphoreType.DMA
    state_shape = shape((heads, BLK, BLK), F32)

    def hold(parts, after):
        return pl.pallas_call(
            join_kernel,
            out_shape=shape((2 * len(parts), 2, BLK, width), BF16),
            in_specs=[VMEM] * len(parts) + [ANY],
            out_specs=VMEM,
            compiler_params=params(4),
            cost_estimate=cost(1, 1),
            name="join",
        )(*parts, after)

    if direct:
        *theirs, their_queries = [flip(x, 1) for x in (keys, values, queries)]
        mine = pl.pallas_call(
            pick_kernel,
            out_shape=shape((4, 2, BLK, width), BF16),
            in_specs=[SMEM] + [HBM] * 2,
            out_specs=VMEM,
            scratch_shapes=[dma],
            compiler_params=params(53),
            cost_estimate=cost(1, 1),
            name="pick",
        )(where, keys, values)
        sent = pl.pallas_call(
            pair_kernel,
            out_shape=[shape((2, 2, BLK, width), BF16)] * 4,
            in_specs=[SMEM] + [VMEM] * 3,
            out_specs=[VMEM] * 4,
            compiler_params=params(4),
            cost_estimate=cost(3*10**9, 1),
            name="pair",
        )(where, mine, *theirs)
        kv = [sent[0]] + [flip(sent[j], 2 * j) for j in range(1, 4)]
        layout = [(j, 0, 2, lambda m, j=j: (m ^ (2 * j)) // 2 * 2) for j in range(4)]
        q_layout = layout
        first = onward(kv[0], 1)
        q = pl.pallas_call(
            pair_queries_kernel,
            out_shape=[shape((2, BLK, width), BF16)] * 4,
            in_specs=[SMEM] + [VMEM] * 2 + [ANY],
            out_specs=[VMEM] * 4,
            compiler_params=params(4),
            cost_estimate=cost(1, 1),
            name="pair_queries",
        )(where, queries, their_queries, kv[0])
        second = onward(hold(kv[1:2], q[1]), 1)
        far = [first, second, onward(kv[2], 1)]
        far_layout = layout
        earlier = [second, first]
        ready = []
        q = [q[0]] + [flip(q[j], 2 * j) for j in range(1, 4)]
    else:
        earlier = []
        ready = []
        def by_heads(parts):
            parts = parts.reshape(-1, tokens // BLK, BLK, group_size, width)
            parts = parts.transpose(3, 1, 0, 2, 4)
            if group_size > 1:
                parts = lax.all_to_all(parts, axis, 0, 0, axis_index_groups=members, tiled=True)
            return parts.reshape(blocks, -1, BLK, width)

        kv = [by_heads(jnp.stack([keys, values]))]
        q = [by_heads(queries)[:, 0]]
        far = [onward(kv[0], distance) for distance in range(WIN // span, 0, -1)]
        layout = q_layout = [(0, 0, blocks, lambda m: 0)]
        ready = []
        far_layout = [(c, 0, blocks, lambda m, c=c: c * blocks) for c in range(len(far))]

    total, before, inject = pl.pallas_call(
        functools.partial(memory_kernel, layout),
        out_shape=[
            shape((heads, BLK, 2 * BLK), BF16),
            shape((blocks, heads, BLK, 2 * BLK), BF16),
            shape((blocks, heads, BLK, 2 * BLK), BF16),
        ],
        in_specs=[SMEM] * 2 + [VMEM] * len(kv) + [ANY] * len(earlier),
        out_specs=[VMEM] * 3,
        scratch_shapes=[pltpu.VMEM((blocks, 2, BLK, width), BF16)],
        compiler_params=params(12),
        cost_estimate=cost(50 * 10**8, 1),
        name="memory_updates",
    )(where, step_rate, *kv, *earlier)

    near, logs, lin, off = pl.pallas_call(
        functools.partial(local_kernel, layout, q_layout),
        out_shape=[
            shape((heads, blocks, BLK, BLK), F32),
            state_shape,
            shape((heads, blocks, BLK, BLK), BF16),
            shape((heads, blocks, BLK, BLK), F32),
        ],
        in_specs=[SMEM] + [VMEM] * (len(kv) + len(q) + 2) + [ANY] * len(ready),
        out_specs=[VMEM] * 4,
        scratch_shapes=[
            pltpu.VMEM((blocks, BLK, width), BF16),
            pltpu.VMEM((blocks, 2, BLK, width), BF16),
        ],
        compiler_params=params(12),
        cost_estimate=cost(40 * 10**8, 1),
        name="attend_own",
    )(where, *kv, *q, before, inject, *ready)
    if direct:
        held = flip(total, group_size)
        far.append(onward(hold(kv[3:], total), 1))
        own, after = pl.pallas_call(
            after_kernel,
            out_shape=[state_shape, shape((heads, BLK, BLK), BF16)],
            in_specs=[SMEM] + [VMEM] * 3 + [ANY],
            out_specs=[VMEM, VMEM],
            compiler_params=params(8),
            cost_estimate=cost(1, 1),
            name="state_after",
        )(where, held, total, memory_init, far[2])
        moved = flip(after, 2 * group_size)
    else:
        updates = lax.all_gather(
            total, axis, axis_index_groups=[list(x) for x in zip(*members)]
        )
        own = pl.pallas_call(
            chain_kernel,
            out_shape=state_shape,
            in_specs=[SMEM, VMEM, HBM],
            out_specs=VMEM,
            scratch_shapes=[dma],
            compiler_params=params(32),
            name="state_chain",
        )(where, updates, memory_init)
        moved, held = own.astype(BF16), total

    attended = pl.pallas_call(
        functools.partial(far_kernel, far_layout, q_layout),
        out_shape=shape((heads, blocks, BLK, BLK), F32),
        in_specs=[SMEM] + [VMEM] * (2 + len(far) + len(q)),
        out_specs=VMEM,
        scratch_shapes=[
            pltpu.VMEM((blocks, BLK, width), BF16),
            pltpu.VMEM((reach, 2, BLK, width), BF16),
        ],
        compiler_params=params(12),
        cost_estimate=cost(4 * 10**9, 1),
        name="attend_far",
    )(where, near, logs, *far, *q)
    gated = pl.pallas_call(
        gate_kernel,
        out_shape=[shape((tokens, width), BF16)] * group_size,
        in_specs=[SMEM] + [VMEM] * 6,
        out_specs=[VMEM] * group_size,
        compiler_params=params(8),
        cost_estimate=cost(10**9, 1),
        name="gate",
    )(where, attended, lin, off, own, moved, held)
    gated = [gated[0]] + [flip(gated[s], s) for s in range(1, group_size)]
    features = out_weight.shape[1]
    split_out = lax.axis_size("tp") > 1
    part = []
    early = list(range(7 if group_size == 8 else 0))
    if early:
        part = [
            pl.pallas_call(
                functools.partial(partial_kernel, early),
                out_shape=shape((tokens, features), F32),
                in_specs=[SMEM] + [VMEM] * (1 + len(early)),
                out_specs=VMEM,
                compiler_params=params(8),
                cost_estimate=cost(10**9, 1),
                name="project_early",
            )(where, out_weight, *[gated[s] for s in early])
        ]
    late = list(range(len(early), group_size))
    kind = F32 if split_out else BF16
    projected = pl.pallas_call(
        functools.partial(project_kernel, late),
        out_shape=shape((tokens, features), kind),
        in_specs=[SMEM] + [VMEM] * (1 + len(late) + len(part)),
        out_specs=HBM,
        scratch_shapes=[pltpu.VMEM((tokens, features), kind), dma],
        compiler_params=params(8),
        cost_estimate=cost(10**9, 1),
        name="project",
    )(where, out_weight, *[gated[s] for s in late], *part)
    if split_out:
        projected = lax.psum_scatter(projected, "tp", scatter_dimension=1, tiled=True)
    return projected.astype(BF16)


def solution(mesh):
    return jax.shard_map(
        shards,
        mesh=mesh,
        in_specs=(
            P("seq", "tp"),
            P("seq", "tp"),
            P("seq", "tp"),
            P("tp"),
            P("tp", None, None),
            P("tp", None),
        ),
        out_specs=P("seq", "tp"),
        check_vma=False,
    )
```

```python
import functools
import math

import jax
import jax.numpy as jnp
from jax import lax
from jax.experimental import pallas as pl
from jax.experimental.pallas import tpu as pltpu
from jax.sharding import PartitionSpec as P

WIN = 1024
CH = 16
BLK = 128
MASKED = -1e30
SCALE = math.log2(math.e) / math.sqrt(BLK)
F32 = jnp.float32
BF16 = jnp.bfloat16


def dot(a, b):
    return jnp.dot(a.astype(BF16), b.astype(BF16), preferred_element_type=F32)


def dot_nt(a, b):
    return lax.dot_general(a, b, (((1,), (1,)), ((), ())), preferred_element_type=F32)


def dot_tn(a, b):
    return lax.dot_general(a, b, (((0,), (0,)), ((), ())), preferred_element_type=F32)


def earlier_chunk():
    row = lax.broadcasted_iota(jnp.int32, (BLK, BLK), 0) // CH
    col = lax.broadcasted_iota(jnp.int32, (BLK, BLK), 1) // CH
    return row, col, col < row


def at(where, index):
    group_size, last_own = where
    position = lax.axis_index("seq")
    return (lax.rem(position, group_size), lax.div(position, group_size), last_own)[index]


def head_columns(member, j, width):
    return pl.ds(pl.multiple_of(lax.bitwise_xor(member, 2 * j) * width, width), width)


def pick_kernel(where_ref, k_ref, v_ref, out_ref, sem):
    copies = []
    for j in range(out_ref.shape[0]):
        columns = head_columns(at(where_ref, 0), j, out_ref.shape[-1])
        for t, source in enumerate((k_ref, v_ref)):
            copies.append(pltpu.make_async_copy(source.at[:, columns], out_ref.at[j, t], sem))
            copies[-1].start()
    wait_all(copies)


def pair_kernel(where_ref, mine_ref, k_ref, v_ref, *outs):
    row = at(where_ref, 0) & 1
    for j, out in enumerate(outs):
        columns = head_columns(at(where_ref, 0), j, out.shape[-1])
        out[pl.ds(row, 1)] = mine_ref[j : j + 1]
        out[pl.ds(1 - row, 1), 0] = k_ref[:, columns][None]
        out[pl.ds(1 - row, 1), 1] = v_ref[:, columns][None]


def pair_queries_kernel(where_ref, mine_ref, theirs_ref, _, *outs):
    row = at(where_ref, 0) & 1
    for j, out in enumerate(outs):
        columns = head_columns(at(where_ref, 0), j, out.shape[-1])
        out[pl.ds(row, 1)] = mine_ref[:, columns][None]
        out[pl.ds(1 - row, 1)] = theirs_ref[:, columns][None]


def join_kernel(*refs):
    parts, out_ref = refs[:-2], refs[-1]
    for i, part in enumerate(parts):
        count = part.shape[0]
        out_ref[i * count : (i + 1) * count] = part[...]


def place_pieces(layout, member, pieces, held_ref):
    for piece, index, count, number in layout:
        held_ref[pl.ds(number(member), count)] = pieces[piece][index : index + count]


def wait_all(copies):
    for copy in copies:
        copy.wait()


def memory_kernel(layout, where_ref, rates_ref, *refs):
    pieces, (total_ref, before_ref, inject_ref, kv_ref) = refs[:-4], refs[-4:]
    blocks = before_ref.shape[0]
    heads = total_ref.shape[0]
    place_pieces(layout, at(where_ref, 0), pieces, kv_ref)
    row, col, strict = earlier_chunk()
    near = strict & (row // 2 == col // 2)
    middle = strict & (row // 4 == col // 4) & (row // 2 != col // 2)
    far = strict & (row // 4 != col // 4)
    eye = (
        lax.broadcasted_iota(jnp.int32, (BLK, BLK), 0)
        == lax.broadcasted_iota(jnp.int32, (BLK, BLK), 1)
    ).astype(F32)
    todo = [(b, h) for b in range(blocks) for h in range(heads)]
    every = range(len(todo))
    rate = [rates_ref[at(where_ref, 0) * heads + h] for _, h in todo]
    k, v = [
        [kv_ref[b, t, :, h * BLK : (h + 1) * BLK] for b, h in todo]
        for t in range(2)
    ]
    kf = [x.astype(F32) for x in k]
    norm = [
        lax.rsqrt(BLK * (jnp.mean(x * x, axis=-1, keepdims=True) + 1e-06)) for x in kf
    ]
    unit = [kf[i] * norm[i] for i in every]
    rounded = [x.astype(BF16) for x in unit]
    lower = [dot_nt(rounded[i], rounded[i]) * rate[i] for i in every]
    half = [-jnp.where(near, x, 0.0) for x in lower]
    for region in (middle, far):
        inv = [(x + eye).astype(BF16) for x in half]
        part = [dot(jnp.where(region, lower[i], 0.0), inv[i]) for i in every]
        half = [half[i] - dot(inv[i], part[i]) for i in every]
    both = [dot(half[i], jnp.concatenate([rounded[i], v[i]], axis=1)) for i in every]
    both = [
        both[i] + jnp.concatenate([unit[i], v[i].astype(F32)], axis=1) for i in every
    ]
    weighted = [(both[i] * (norm[i] * rate[i])).astype(BF16) for i in every]
    for i, (b, h) in enumerate(todo):
        inject_ref[b, h] = weighted[i]
    change = [dot_tn(k[i], weighted[i]) for i in every]
    running = [jnp.concatenate([eye, jnp.zeros_like(eye)], axis=1) for _ in range(heads)]
    for i, (b, h) in enumerate(todo):
        before = running[h].astype(BF16)
        before_ref[b, h] = before
        after = running[h] - dot(change[i][:, :BLK], before)
        running[h] = jnp.concatenate(
            [after[:, :BLK], after[:, BLK:] + change[i][:, BLK:]], axis=1
        )
    for h in range(heads):
        total_ref[h] = running[h].astype(BF16)


def own_state(where_ref, init_hbm, init_ref, sem):
    heads = init_ref.shape[0]
    copy = pltpu.make_async_copy(init_hbm.at[pl.ds(at(where_ref, 0) * heads, heads)], init_ref, sem)
    copy.start()
    return copy


def advance(update, state):
    return dot(update[:, :BLK], state) + update[:, BLK:].astype(F32)


def after_kernel(where_ref, held_ref, total_ref, init_ref, *refs):
    own_ref, after_ref = refs[-2:]
    heads = own_ref.shape[0]
    second = at(where_ref, 1) % 2 == 1
    for h in range(after_ref.shape[0]):
        state = init_ref[at(where_ref, 0) * heads + h]
        earlier = advance(jnp.where(second, held_ref[h], total_ref[h]), state)
        own_ref[h] = jnp.where(second, earlier, state)
        later = jnp.where(second, total_ref[h], held_ref[h])
        after_ref[h] = advance(later, earlier).astype(BF16)


def chain_kernel(where_ref, updates_ref, init_hbm, state_ref, sem):
    own_state(where_ref, init_hbm, state_ref, sem).wait()

    @pl.loop(0, at(where_ref, 1))
    def _(g):
        for h in range(state_ref.shape[0]):
            state_ref[h] = advance(updates_ref[g, h], state_ref[h])


def within_block():
    row = lax.broadcasted_iota(jnp.int32, (BLK, BLK), 0)
    col = lax.broadcasted_iota(jnp.int32, (BLK, BLK), 1)
    return row, col


def weigh(p, v):
    return jnp.dot(p, jnp.concatenate([v, jnp.ones_like(v)], axis=1), preferred_element_type=F32)


def batches(blocks, heads, count):
    todo = [(b, h) for b in range(blocks) for h in range(heads)]
    return [todo[i : i + count] for i in range(0, len(todo), count)]


def local_kernel(kv_layout, q_layout, where_ref, *refs):
    kv_pieces = refs[: len(kv_layout)]
    q_pieces = refs[len(kv_layout) : len(kv_layout) + len(q_layout)]
    before_ref, inject_ref = refs[len(kv_layout) + len(q_layout) :][:2]
    attended_ref, logs_ref, lin_ref, off_ref, q_ref, kv_ref = refs[-6:]
    blocks = kv_ref.shape[0]
    heads = attended_ref.shape[0]
    place_pieces(q_layout, at(where_ref, 0), q_pieces, q_ref)
    place_pieces(kv_layout, at(where_ref, 0), kv_pieces, kv_ref)
    row, col = within_block()
    logs = [jnp.zeros((BLK, BLK), F32) for _ in range(heads)]
    strict = earlier_chunk()[2]
    todo = [(b, h) for b in range(blocks) for h in range(heads)]
    every = range(len(todo))
    q = [q_ref[b, :, h * BLK : (h + 1) * BLK] for b, h in todo]
    diagonal = [
        dot_nt(q[i], kv_ref[b, 0, :, h * BLK : (h + 1) * BLK]) for i, (b, h) in enumerate(todo)
    ]
    inner = [jnp.where(strict, s, 0.0) for s in diagonal]
    inside = [dot(inner[i], inject_ref[b, h]) for i, (b, h) in enumerate(todo)]
    scores = []
    for i, (b, h) in enumerate(todo):
        s = jnp.where(col <= row, diagonal[i], MASKED)
        if b > 0:
            k = kv_ref[0:b, 0, :, h * BLK : (h + 1) * BLK].reshape(b * BLK, BLK)
            s = jnp.concatenate([dot_nt(q[i], k), s], axis=1)
        scores.append(s)
    rows = [
        dot(q[i].astype(F32) - inside[i][:, :BLK], before_ref[b, h])
        for i, (b, h) in enumerate(todo)
    ]
    for i, (b, h) in enumerate(todo):
        lin_ref[h, b] = rows[i][:, :BLK].astype(BF16)
        off_ref[h, b] = rows[i][:, BLK:] + inside[i][:, BLK:]
    top = [jnp.max(s, axis=-1, keepdims=True) * SCALE for s in scores]
    p = [jnp.exp2(s * SCALE - t).astype(BF16) for s, t in zip(scores, top)]
    for i, (b, h) in enumerate(todo):
        v = kv_ref[0 : b + 1, 1, :, h * BLK : (h + 1) * BLK].reshape((b + 1) * BLK, BLK)
        acc = weigh(p[i], v)
        total = acc[:, BLK:]
        attended_ref[h, b] = acc[:, :BLK] / total
        logs[h] = jnp.where(col == b, jnp.log2(total) + top[i], logs[h])
    for h in range(heads):
        logs_ref[h] = logs[h]


def far_kernel(layout, q_layout, where_ref, near_ref, logs_ref, *refs):
    pieces, q_pieces = refs[: -3 - len(q_layout)], refs[-3 - len(q_layout) : -3]
    out_ref, q_ref, kv_ref = refs[-3:]
    reach = kv_ref.shape[0]
    blocks = q_ref.shape[0]
    place_pieces(q_layout, at(where_ref, 0), q_pieces, q_ref)
    place_pieces(layout, at(where_ref, 0), pieces, kv_ref)
    row, col = within_block()
    whole = blocks == reach
    hidden = [
        jnp.where(at(where_ref, 1) * blocks + c < reach, MASKED, 0.0) for c in range(reach)
    ]
    for part in batches(blocks, near_ref.shape[0], 4):
        scores = []
        for b, h in part:
            columns = slice(h * BLK, (h + 1) * BLK)
            k = kv_ref[b:reach, 0, :, columns].reshape((reach - b) * BLK, BLK)
            s = dot_nt(q_ref[b, :, columns], k)
            s = [s[:, i * BLK : (i + 1) * BLK] for i in range(reach - b)]
            if not whole:
                s = [x + hidden[b + i] for i, x in enumerate(s)]
            s[0] = jnp.where(col > row, s[0], MASKED)
            scores.append(jnp.concatenate(s, axis=1) if len(s) > 1 else s[0])
        old = [logs_ref[h][:, b : b + 1] for b, h in part]
        top = [
            jnp.maximum(jnp.max(s, axis=-1, keepdims=True) * SCALE, t)
            for s, t in zip(scores, old)
        ]
        p = [jnp.exp2(s * SCALE - t).astype(BF16) for s, t in zip(scores, top)]
        kept = [jnp.exp2(o - t) for o, t in zip(old, top)]
        for i, (b, h) in enumerate(part):
            columns = slice(h * BLK, (h + 1) * BLK)
            v = kv_ref[b:reach, 1, :, columns].reshape((reach - b) * BLK, BLK)
            acc = weigh(p[i], v)
            sums = acc[:, :BLK] + near_ref[h, b] * kept[i]
            sums = sums / (acc[:, BLK:] + kept[i])
            if whole:
                sums = jnp.where(at(where_ref, 1) == 0, near_ref[h, b], sums)
            out_ref[h, b] = sums


def gate_kernel(where_ref, attended_ref, lin_ref, off_ref, own_ref, moved_ref, held_ref, *refs):
    outs = refs
    heads, blocks = lin_ref.shape[:2]
    count = blocks // len(outs)
    late = at(where_ref, 1) > at(where_ref, 2)
    odd = at(where_ref, 1) % 2 == 1
    state = []
    for h in range(heads):
        moved = moved_ref[h].astype(F32)
        moved = jnp.where(odd, advance(held_ref[h], moved), moved)
        state.append(jnp.where(late, moved, own_ref[h]).astype(BF16))
    numbers = [lax.bitwise_xor(at(where_ref, 0), s) * count for s in range(len(outs))]
    todo = [(s, i, h) for s in range(len(outs)) for i in range(count) for h in range(heads)]
    read = [
        dot(lin_ref[h, numbers[s] + i], state[h]) + off_ref[h, numbers[s] + i]
        for s, i, h in todo
    ]
    for (s, i, h), r in zip(todo, read):
        gated = attended_ref[h, numbers[s] + i] * jax.nn.sigmoid(r)
        rows = slice(i * BLK, (i + 1) * BLK)
        outs[s][rows, h * BLK : (h + 1) * BLK] = gated.astype(BF16)


def project_kernel(place, where_ref, w_ref, *refs):
    pieces, before = refs[: len(place)], refs[len(place) : -3]
    out_ref, held_ref, sem = refs[-3:]
    width = pieces[0].shape[1]
    rows = [
        pl.ds(pl.multiple_of(lax.bitwise_xor(at(where_ref, 0), s) * width, width), width)
        for s in place
    ]
    tile = math.gcd(out_ref.shape[1], 256)
    stores = []
    for start in range(0, out_ref.shape[1], tile):
        columns = pl.ds(start, tile)
        acc = before[0][:, columns] if before else jnp.zeros((out_ref.shape[0], tile), F32)
        for row, piece in zip(rows, pieces):
            acc += jnp.dot(piece[...], w_ref[row, columns], preferred_element_type=F32)
        held_ref[:, columns] = acc.astype(out_ref.dtype)
        stores.append(
            pltpu.make_async_copy(held_ref.at[:, columns], out_ref.at[:, columns], sem)
        )
        stores[-1].start()
    wait_all(stores)


def partial_kernel(place, where_ref, w_ref, *refs):
    pieces, out_ref = refs[:-1], refs[-1]
    width = pieces[0].shape[1]
    acc = jnp.zeros(out_ref.shape, F32)
    for s, piece in zip(place, pieces):
        first = pl.multiple_of(lax.bitwise_xor(at(where_ref, 0), s) * width, width)
        acc += jnp.dot(piece[...], w_ref[pl.ds(first, width), :], preferred_element_type=F32)
    out_ref[...] = acc


VMEM = pl.BlockSpec(memory_space=pltpu.VMEM)
ANY = pl.BlockSpec(memory_space=pl.ANY)
HBM = pl.BlockSpec(memory_space=pltpu.HBM)
SMEM = pl.BlockSpec(memory_space=pltpu.SMEM)


def params(mebibytes):
    return pltpu.CompilerParams(vmem_limit_bytes=mebibytes * 1024 * 1024)


def cost(flops, moved):
    return pl.CostEstimate(flops=flops, bytes_accessed=moved, transcendentals=0)


def shape(dims, kind):
    return jax.ShapeDtypeStruct(dims, kind)


def shards(queries, keys, values, step_rate, memory_init, out_weight):
    axis = "seq"
    size = lax.axis_size(axis)
    place = lax.axis_index(axis).astype(jnp.int32)
    tokens, _ = queries.shape
    local_heads = memory_init.shape[0]
    group_size = math.gcd(local_heads, size, WIN // tokens)
    groups = size // group_size
    heads = local_heads // group_size
    width = heads * BLK
    span = tokens * group_size
    blocks = span // BLK
    reach = WIN // BLK
    members = [[g * group_size + i for i in range(group_size)] for g in range(groups)]
    member = place % group_size
    group = place // group_size
    direct = group_size == 8 and span == WIN and tokens == BLK and groups == 4

    def flip(x, mask):
        return lax.ppermute(x, axis, [(i, i ^ mask) for i in range(size)])

    def onward(x, distance):
        shift = distance * group_size
        return lax.ppermute(x, axis, [(i, i + shift) for i in range(size - shift)])

    last_own = 1 if direct else groups
    where = (group_size, last_own)
    dma = pltpu.SemaphoreType.DMA
    state_shape = shape((heads, BLK, BLK), F32)

    def hold(parts, after):
        return pl.pallas_call(
            join_kernel,
            out_shape=shape((2 * len(parts), 2, BLK, width), BF16),
            in_specs=[VMEM] * len(parts) + [ANY],
            out_specs=VMEM,
            compiler_params=params(4),
            cost_estimate=cost(1, 1),
            name="join",
        )(*parts, after)

    if direct:
        *theirs, their_queries = [flip(x, 1) for x in (keys, values, queries)]
        mine = pl.pallas_call(
            functools.partial(pick_kernel, where),
            out_shape=shape((4, 2, BLK, width), BF16),
            in_specs=[HBM] * 2,
            out_specs=VMEM,
            scratch_shapes=[dma],
            compiler_params=params(53),
            cost_estimate=cost(1, 1),
            name="pick",
        )(keys, values)
        sent = pl.pallas_call(
            functools.partial(pair_kernel, where),
            out_shape=[shape((2, 2, BLK, width), BF16)] * 4,
            in_specs=[VMEM] * 3,
            out_specs=[VMEM] * 4,
            compiler_params=params(4),
            cost_estimate=cost(3*10**9, 1),
            name="pair",
        )(mine, *theirs)
        kv = [sent[0]] + [flip(sent[j], 2 * j) for j in range(1, 4)]
        layout = [(j, 0, 2, lambda m, j=j: (m ^ (2 * j)) // 2 * 2) for j in range(4)]
        q_layout = layout
        first = onward(kv[0], 1)
        q = pl.pallas_call(
            functools.partial(pair_queries_kernel, where),
            out_shape=[shape((2, BLK, width), BF16)] * 4,
            in_specs=[VMEM] * 2 + [ANY],
            out_specs=[VMEM] * 4,
            compiler_params=params(4),
            cost_estimate=cost(1, 1),
            name="pair_queries",
        )(queries, their_queries, kv[0])
        second = onward(hold(kv[1:2], q[1]), 1)
        far = [first, second, onward(kv[2], 1)]
        far_layout = layout
        earlier = [second, first]
        ready = []
        q = [q[0]] + [flip(q[j], 2 * j) for j in range(1, 4)]
    else:
        earlier = []
        ready = []
        def by_heads(parts):
            parts = parts.reshape(-1, tokens // BLK, BLK, group_size, width)
            parts = parts.transpose(3, 1, 0, 2, 4)
            if group_size > 1:
                parts = lax.all_to_all(parts, axis, 0, 0, axis_index_groups=members, tiled=True)
            return parts.reshape(blocks, -1, BLK, width)

        kv = [by_heads(jnp.stack([keys, values]))]
        q = [by_heads(queries)[:, 0]]
        far = [onward(kv[0], distance) for distance in range(WIN // span, 0, -1)]
        layout = q_layout = [(0, 0, blocks, lambda m: 0)]
        ready = []
        far_layout = [(c, 0, blocks, lambda m, c=c: c * blocks) for c in range(len(far))]

    total, before, inject = pl.pallas_call(
        functools.partial(memory_kernel, layout, where),
        out_shape=[
            shape((heads, BLK, 2 * BLK), BF16),
            shape((blocks, heads, BLK, 2 * BLK), BF16),
            shape((blocks, heads, BLK, 2 * BLK), BF16),
        ],
        in_specs=[SMEM] + [VMEM] * len(kv) + [ANY] * len(earlier),
        out_specs=[VMEM] * 3,
        scratch_shapes=[pltpu.VMEM((blocks, 2, BLK, width), BF16)],
        compiler_params=params(12),
        cost_estimate=cost(50 * 10**8, 1),
        name="memory_updates",
    )(step_rate, *kv, *earlier)

    near, logs, lin, off = pl.pallas_call(
        functools.partial(local_kernel, layout, q_layout, where),
        out_shape=[
            shape((heads, blocks, BLK, BLK), F32),
            state_shape,
            shape((heads, blocks, BLK, BLK), BF16),
            shape((heads, blocks, BLK, BLK), F32),
        ],
        in_specs=[VMEM] * (len(kv) + len(q) + 2) + [ANY] * len(ready),
        out_specs=[VMEM] * 4,
        scratch_shapes=[
            pltpu.VMEM((blocks, BLK, width), BF16),
            pltpu.VMEM((blocks, 2, BLK, width), BF16),
        ],
        compiler_params=params(12),
        cost_estimate=cost(40 * 10**8, 1),
        name="attend_own",
    )(*kv, *q, before, inject, *ready)
    if direct:
        held = flip(total, group_size)
        far.append(onward(hold(kv[3:], total), 1))
        own, after = pl.pallas_call(
            functools.partial(after_kernel, where),
            out_shape=[state_shape, shape((heads, BLK, BLK), BF16)],
            in_specs=[VMEM] * 3 + [ANY],
            out_specs=[VMEM, VMEM],
            compiler_params=params(8),
            cost_estimate=cost(1, 1),
            name="state_after",
        )(held, total, memory_init, far[2])
        moved = flip(after, 2 * group_size)
    else:
        updates = lax.all_gather(
            total, axis, axis_index_groups=[list(x) for x in zip(*members)]
        )
        own = pl.pallas_call(
            functools.partial(chain_kernel, where),
            out_shape=state_shape,
            in_specs=[VMEM, HBM],
            out_specs=VMEM,
            scratch_shapes=[dma],
            compiler_params=params(32),
            name="state_chain",
        )(updates, memory_init)
        moved, held = own.astype(BF16), total

    attended = pl.pallas_call(
        functools.partial(far_kernel, far_layout, q_layout, where),
        out_shape=shape((heads, blocks, BLK, BLK), F32),
        in_specs=[VMEM] * (2 + len(far) + len(q)),
        out_specs=VMEM,
        scratch_shapes=[
            pltpu.VMEM((blocks, BLK, width), BF16),
            pltpu.VMEM((reach, 2, BLK, width), BF16),
        ],
        compiler_params=params(12),
        cost_estimate=cost(4 * 10**9, 1),
        name="attend_far",
    )(near, logs, *far, *q)
    gated = pl.pallas_call(
        functools.partial(gate_kernel, where),
        out_shape=[shape((tokens, width), BF16)] * group_size,
        in_specs=[VMEM] * 6,
        out_specs=[VMEM] * group_size,
        compiler_params=params(8),
        cost_estimate=cost(10**9, 1),
        name="gate",
    )(attended, lin, off, own, moved, held)
    gated = [gated[0]] + [flip(gated[s], s) for s in range(1, group_size)]
    features = out_weight.shape[1]
    split_out = lax.axis_size("tp") > 1
    part = []
    early = list(range(7 if group_size == 8 else 0))
    if early:
        part = [
            pl.pallas_call(
                functools.partial(partial_kernel, early, where),
                out_shape=shape((tokens, features), F32),
                in_specs=[VMEM] * (1 + len(early)),
                out_specs=VMEM,
                compiler_params=params(8),
                cost_estimate=cost(10**9, 1),
                name="project_early",
            )(out_weight, *[gated[s] for s in early])
        ]
    late = list(range(len(early), group_size))
    kind = F32 if split_out else BF16
    projected = pl.pallas_call(
        functools.partial(project_kernel, late, where),
        out_shape=shape((tokens, features), kind),
        in_specs=[VMEM] * (1 + len(late) + len(part)),
        out_specs=HBM,
        scratch_shapes=[pltpu.VMEM((tokens, features), kind), dma],
        compiler_params=params(8),
        cost_estimate=cost(10**9, 1),
        name="project",
    )(out_weight, *[gated[s] for s in late], *part)
    if split_out:
        projected = lax.psum_scatter(projected, "tp", scatter_dimension=1, tiled=True)
    return projected.astype(BF16)


def solution(mesh):
    return jax.shard_map(
        shards,
        mesh=mesh,
        in_specs=(
            P("seq", "tp"),
            P("seq", "tp"),
            P("seq", "tp"),
            P("tp"),
            P("tp", None, None),
            P("tp", None),
        ),
        out_specs=P("seq", "tp"),
        check_vma=False,
    )
```

```python
import functools
import math

import jax
import jax.numpy as jnp
from jax import lax
from jax.experimental import pallas as pl
from jax.experimental.pallas import tpu as pltpu
from jax.sharding import PartitionSpec as P

WIN = 1024
CH = 16
BLK = 128
MASKED = -1e30
SCALE = math.log2(math.e) / math.sqrt(BLK)
F32 = jnp.float32
BF16 = jnp.bfloat16


def dot(a, b):
    return jnp.dot(a.astype(BF16), b.astype(BF16), preferred_element_type=F32)


def dot_nt(a, b):
    return lax.dot_general(a, b, (((1,), (1,)), ((), ())), preferred_element_type=F32)


def dot_tn(a, b):
    return lax.dot_general(a, b, (((0,), (0,)), ((), ())), preferred_element_type=F32)


def earlier_chunk():
    row = lax.broadcasted_iota(jnp.int32, (BLK, BLK), 0) // CH
    col = lax.broadcasted_iota(jnp.int32, (BLK, BLK), 1) // CH
    return row, col, col < row


def at(where, index):
    group_size, last_own = where
    position = lax.axis_index("seq")
    return (lax.rem(position, group_size), lax.div(position, group_size), last_own)[index]


def head_columns(member, j, width):
    return pl.ds(pl.multiple_of(lax.bitwise_xor(member, 2 * j) * width, width), width)


def pick_kernel(where_ref, k_ref, v_ref, out_ref, sem):
    copies = []
    for j in range(out_ref.shape[0]):
        columns = head_columns(at(where_ref, 0), j, out_ref.shape[-1])
        for t, source in enumerate((k_ref, v_ref)):
            copies.append(pltpu.make_async_copy(source.at[:, columns], out_ref.at[j, t], sem))
            copies[-1].start()
    wait_all(copies)


def pair_kernel(where_ref, mine_ref, k_ref, v_ref, *outs):
    row = at(where_ref, 0) & 1
    for j, out in enumerate(outs):
        columns = head_columns(at(where_ref, 0), j, out.shape[-1])
        out[pl.ds(row, 1)] = mine_ref[j : j + 1]
        out[pl.ds(1 - row, 1), 0] = k_ref[:, columns][None]
        out[pl.ds(1 - row, 1), 1] = v_ref[:, columns][None]


def pair_queries_kernel(where_ref, rates_ref, mine_ref, theirs_ref, _, *refs):
    outs, rates_out = refs[:-1], refs[-1]
    heads = rates_out.shape[0]
    for h in range(heads):
        rate = rates_ref[at(where_ref, 0) * heads + h]
        rates_out[h] = jnp.full(rates_out.shape[1:], rate, F32)
    row = at(where_ref, 0) & 1
    for j, out in enumerate(outs):
        columns = head_columns(at(where_ref, 0), j, out.shape[-1])
        out[pl.ds(row, 1)] = mine_ref[:, columns][None]
        out[pl.ds(1 - row, 1)] = theirs_ref[:, columns][None]


def join_kernel(*refs):
    parts, out_ref = refs[:-2], refs[-1]
    for i, part in enumerate(parts):
        count = part.shape[0]
        out_ref[i * count : (i + 1) * count] = part[...]


def place_pieces(layout, member, pieces, held_ref):
    for piece, index, count, number in layout:
        held_ref[pl.ds(number(member), count)] = pieces[piece][index : index + count]


def wait_all(copies):
    for copy in copies:
        copy.wait()


def memory_kernel(layout, where_ref, rates_ref, *refs):
    pieces, (total_ref, before_ref, inject_ref, kv_ref) = refs[:-4], refs[-4:]
    blocks = before_ref.shape[0]
    heads = total_ref.shape[0]
    place_pieces(layout, at(where_ref, 0), pieces, kv_ref)
    row, col, strict = earlier_chunk()
    near = strict & (row // 2 == col // 2)
    middle = strict & (row // 4 == col // 4) & (row // 2 != col // 2)
    far = strict & (row // 4 != col // 4)
    eye = (
        lax.broadcasted_iota(jnp.int32, (BLK, BLK), 0)
        == lax.broadcasted_iota(jnp.int32, (BLK, BLK), 1)
    ).astype(F32)
    todo = [(b, h) for b in range(blocks) for h in range(heads)]
    every = range(len(todo))
    rate = [rates_ref[h][:1] for _, h in todo]
    k, v = [
        [kv_ref[b, t, :, h * BLK : (h + 1) * BLK] for b, h in todo]
        for t in range(2)
    ]
    kf = [x.astype(F32) for x in k]
    norm = [
        lax.rsqrt(BLK * (jnp.mean(x * x, axis=-1, keepdims=True) + 1e-06)) for x in kf
    ]
    unit = [kf[i] * norm[i] for i in every]
    rounded = [x.astype(BF16) for x in unit]
    lower = [dot_nt(rounded[i], rounded[i]) * rate[i] for i in every]
    half = [-jnp.where(near, x, 0.0) for x in lower]
    for region in (middle, far):
        inv = [(x + eye).astype(BF16) for x in half]
        part = [dot(jnp.where(region, lower[i], 0.0), inv[i]) for i in every]
        half = [half[i] - dot(inv[i], part[i]) for i in every]
    both = [dot(half[i], jnp.concatenate([rounded[i], v[i]], axis=1)) for i in every]
    both = [
        both[i] + jnp.concatenate([unit[i], v[i].astype(F32)], axis=1) for i in every
    ]
    weighted = [(both[i] * (norm[i] * rate[i][:, :1])).astype(BF16) for i in every]
    for i, (b, h) in enumerate(todo):
        inject_ref[b, h] = weighted[i]
    change = [dot_tn(k[i], weighted[i]) for i in every]
    running = [jnp.concatenate([eye, jnp.zeros_like(eye)], axis=1) for _ in range(heads)]
    for i, (b, h) in enumerate(todo):
        before = running[h].astype(BF16)
        before_ref[b, h] = before
        after = running[h] - dot(change[i][:, :BLK], before)
        running[h] = jnp.concatenate(
            [after[:, :BLK], after[:, BLK:] + change[i][:, BLK:]], axis=1
        )
    for h in range(heads):
        total_ref[h] = running[h].astype(BF16)


def own_state(where_ref, init_hbm, init_ref, sem):
    heads = init_ref.shape[0]
    copy = pltpu.make_async_copy(init_hbm.at[pl.ds(at(where_ref, 0) * heads, heads)], init_ref, sem)
    copy.start()
    return copy


def advance(update, state):
    return dot(update[:, :BLK], state) + update[:, BLK:].astype(F32)


def after_kernel(where_ref, held_ref, total_ref, init_ref, *refs):
    own_ref, after_ref = refs[-2:]
    heads = own_ref.shape[0]
    second = at(where_ref, 1) % 2 == 1
    for h in range(after_ref.shape[0]):
        state = init_ref[at(where_ref, 0) * heads + h]
        earlier = advance(jnp.where(second, held_ref[h], total_ref[h]), state)
        own_ref[h] = jnp.where(second, earlier, state)
        later = jnp.where(second, total_ref[h], held_ref[h])
        after_ref[h] = advance(later, earlier).astype(BF16)


def chain_kernel(where_ref, updates_ref, init_hbm, state_ref, sem):
    own_state(where_ref, init_hbm, state_ref, sem).wait()

    @pl.loop(0, at(where_ref, 1))
    def _(g):
        for h in range(state_ref.shape[0]):
            state_ref[h] = advance(updates_ref[g, h], state_ref[h])


def within_block():
    row = lax.broadcasted_iota(jnp.int32, (BLK, BLK), 0)
    col = lax.broadcasted_iota(jnp.int32, (BLK, BLK), 1)
    return row, col


def weigh(p, v):
    return jnp.dot(p, jnp.concatenate([v, jnp.ones_like(v)], axis=1), preferred_element_type=F32)


def batches(blocks, heads, count):
    todo = [(b, h) for b in range(blocks) for h in range(heads)]
    return [todo[i : i + count] for i in range(0, len(todo), count)]


def local_kernel(kv_layout, q_layout, where_ref, *refs):
    kv_pieces = refs[: len(kv_layout)]
    q_pieces = refs[len(kv_layout) : len(kv_layout) + len(q_layout)]
    before_ref, inject_ref = refs[len(kv_layout) + len(q_layout) :][:2]
    attended_ref, logs_ref, lin_ref, off_ref, q_ref, kv_ref = refs[-6:]
    blocks = kv_ref.shape[0]
    heads = attended_ref.shape[0]
    place_pieces(q_layout, at(where_ref, 0), q_pieces, q_ref)
    place_pieces(kv_layout, at(where_ref, 0), kv_pieces, kv_ref)
    row, col = within_block()
    logs = [jnp.zeros((BLK, BLK), F32) for _ in range(heads)]
    strict = earlier_chunk()[2]
    todo = [(b, h) for b in range(blocks) for h in range(heads)]
    every = range(len(todo))
    q = [q_ref[b, :, h * BLK : (h + 1) * BLK] for b, h in todo]
    diagonal = [
        dot_nt(q[i], kv_ref[b, 0, :, h * BLK : (h + 1) * BLK]) for i, (b, h) in enumerate(todo)
    ]
    inner = [jnp.where(strict, s, 0.0) for s in diagonal]
    inside = [dot(inner[i], inject_ref[b, h]) for i, (b, h) in enumerate(todo)]
    scores = []
    for i, (b, h) in enumerate(todo):
        s = jnp.where(col <= row, diagonal[i], MASKED)
        if b > 0:
            k = kv_ref[0:b, 0, :, h * BLK : (h + 1) * BLK].reshape(b * BLK, BLK)
            s = jnp.concatenate([dot_nt(q[i], k), s], axis=1)
        scores.append(s)
    rows = [
        dot(q[i].astype(F32) - inside[i][:, :BLK], before_ref[b, h])
        for i, (b, h) in enumerate(todo)
    ]
    for i, (b, h) in enumerate(todo):
        lin_ref[h, b] = rows[i][:, :BLK].astype(BF16)
        off_ref[h, b] = rows[i][:, BLK:] + inside[i][:, BLK:]
    top = [jnp.max(s, axis=-1, keepdims=True) * SCALE for s in scores]
    p = [jnp.exp2(s * SCALE - t).astype(BF16) for s, t in zip(scores, top)]
    for i, (b, h) in enumerate(todo):
        v = kv_ref[0 : b + 1, 1, :, h * BLK : (h + 1) * BLK].reshape((b + 1) * BLK, BLK)
        acc = weigh(p[i], v)
        total = acc[:, BLK:]
        attended_ref[h, b] = acc[:, :BLK] / total
        logs[h] = jnp.where(col == b, jnp.log2(total) + top[i], logs[h])
    for h in range(heads):
        logs_ref[h] = logs[h]


def far_kernel(layout, q_layout, where_ref, near_ref, logs_ref, *refs):
    pieces, q_pieces = refs[: -3 - len(q_layout)], refs[-3 - len(q_layout) : -3]
    out_ref, q_ref, kv_ref = refs[-3:]
    reach = kv_ref.shape[0]
    blocks = q_ref.shape[0]
    place_pieces(q_layout, at(where_ref, 0), q_pieces, q_ref)
    place_pieces(layout, at(where_ref, 0), pieces, kv_ref)
    row, col = within_block()
    whole = blocks == reach
    hidden = [
        jnp.where(at(where_ref, 1) * blocks + c < reach, MASKED, 0.0) for c in range(reach)
    ]
    for part in batches(blocks, near_ref.shape[0], 4):
        scores = []
        for b, h in part:
            columns = slice(h * BLK, (h + 1) * BLK)
            k = kv_ref[b:reach, 0, :, columns].reshape((reach - b) * BLK, BLK)
            s = dot_nt(q_ref[b, :, columns], k)
            s = [s[:, i * BLK : (i + 1) * BLK] for i in range(reach - b)]
            if not whole:
                s = [x + hidden[b + i] for i, x in enumerate(s)]
            s[0] = jnp.where(col > row, s[0], MASKED)
            scores.append(jnp.concatenate(s, axis=1) if len(s) > 1 else s[0])
        old = [logs_ref[h][:, b : b + 1] for b, h in part]
        top = [
            jnp.maximum(jnp.max(s, axis=-1, keepdims=True) * SCALE, t)
            for s, t in zip(scores, old)
        ]
        p = [jnp.exp2(s * SCALE - t).astype(BF16) for s, t in zip(scores, top)]
        kept = [jnp.exp2(o - t) for o, t in zip(old, top)]
        for i, (b, h) in enumerate(part):
            columns = slice(h * BLK, (h + 1) * BLK)
            v = kv_ref[b:reach, 1, :, columns].reshape((reach - b) * BLK, BLK)
            acc = weigh(p[i], v)
            sums = acc[:, :BLK] + near_ref[h, b] * kept[i]
            sums = sums / (acc[:, BLK:] + kept[i])
            if whole:
                sums = jnp.where(at(where_ref, 1) == 0, near_ref[h, b], sums)
            out_ref[h, b] = sums


def gate_kernel(where_ref, attended_ref, lin_ref, off_ref, own_ref, moved_ref, held_ref, *refs):
    outs = refs
    heads, blocks = lin_ref.shape[:2]
    count = blocks // len(outs)
    late = at(where_ref, 1) > at(where_ref, 2)
    odd = at(where_ref, 1) % 2 == 1
    state = []
    for h in range(heads):
        moved = moved_ref[h].astype(F32)
        moved = jnp.where(odd, advance(held_ref[h], moved), moved)
        state.append(jnp.where(late, moved, own_ref[h]).astype(BF16))
    numbers = [lax.bitwise_xor(at(where_ref, 0), s) * count for s in range(len(outs))]
    todo = [(s, i, h) for s in range(len(outs)) for i in range(count) for h in range(heads)]
    read = [
        dot(lin_ref[h, numbers[s] + i], state[h]) + off_ref[h, numbers[s] + i]
        for s, i, h in todo
    ]
    for (s, i, h), r in zip(todo, read):
        gated = attended_ref[h, numbers[s] + i] * jax.nn.sigmoid(r)
        rows = slice(i * BLK, (i + 1) * BLK)
        outs[s][rows, h * BLK : (h + 1) * BLK] = gated.astype(BF16)


def project_kernel(place, where_ref, w_ref, *refs):
    pieces, before = refs[: len(place)], refs[len(place) : -3]
    out_ref, held_ref, sem = refs[-3:]
    width = pieces[0].shape[1]
    rows = [
        pl.ds(pl.multiple_of(lax.bitwise_xor(at(where_ref, 0), s) * width, width), width)
        for s in place
    ]
    tile = math.gcd(out_ref.shape[1], 256)
    stores = []
    for start in range(0, out_ref.shape[1], tile):
        columns = pl.ds(start, tile)
        acc = before[0][:, columns] if before else jnp.zeros((out_ref.shape[0], tile), F32)
        for row, piece in zip(rows, pieces):
            acc += jnp.dot(piece[...], w_ref[row, columns], preferred_element_type=F32)
        held_ref[:, columns] = acc.astype(out_ref.dtype)
        stores.append(
            pltpu.make_async_copy(held_ref.at[:, columns], out_ref.at[:, columns], sem)
        )
        stores[-1].start()
    wait_all(stores)


def partial_kernel(place, where_ref, w_ref, *refs):
    pieces, out_ref = refs[:-1], refs[-1]
    width = pieces[0].shape[1]
    acc = jnp.zeros(out_ref.shape, F32)
    for s, piece in zip(place, pieces):
        first = pl.multiple_of(lax.bitwise_xor(at(where_ref, 0), s) * width, width)
        acc += jnp.dot(piece[...], w_ref[pl.ds(first, width), :], preferred_element_type=F32)
    out_ref[...] = acc


VMEM = pl.BlockSpec(memory_space=pltpu.VMEM)
ANY = pl.BlockSpec(memory_space=pl.ANY)
HBM = pl.BlockSpec(memory_space=pltpu.HBM)
SMEM = pl.BlockSpec(memory_space=pltpu.SMEM)


def params(mebibytes):
    return pltpu.CompilerParams(vmem_limit_bytes=mebibytes * 1024 * 1024)


def cost(flops, moved):
    return pl.CostEstimate(flops=flops, bytes_accessed=moved, transcendentals=0)


def shape(dims, kind):
    return jax.ShapeDtypeStruct(dims, kind)


def shards(queries, keys, values, step_rate, memory_init, out_weight):
    axis = "seq"
    size = lax.axis_size(axis)
    place = lax.axis_index(axis).astype(jnp.int32)
    tokens, _ = queries.shape
    local_heads = memory_init.shape[0]
    group_size = math.gcd(local_heads, size, WIN // tokens)
    groups = size // group_size
    heads = local_heads // group_size
    width = heads * BLK
    span = tokens * group_size
    blocks = span // BLK
    reach = WIN // BLK
    members = [[g * group_size + i for i in range(group_size)] for g in range(groups)]
    member = place % group_size
    group = place // group_size
    direct = group_size == 8 and span == WIN and tokens == BLK and groups == 4

    def flip(x, mask):
        return lax.ppermute(x, axis, [(i, i ^ mask) for i in range(size)])

    def onward(x, distance):
        shift = distance * group_size
        return lax.ppermute(x, axis, [(i, i + shift) for i in range(size - shift)])

    last_own = 1 if direct else groups
    where = (group_size, last_own)
    dma = pltpu.SemaphoreType.DMA
    state_shape = shape((heads, BLK, BLK), F32)

    def hold(parts, after):
        return pl.pallas_call(
            join_kernel,
            out_shape=shape((2 * len(parts), 2, BLK, width), BF16),
            in_specs=[VMEM] * len(parts) + [ANY],
            out_specs=VMEM,
            compiler_params=params(4),
            cost_estimate=cost(1, 1),
            name="join",
        )(*parts, after)

    if direct:
        *theirs, their_queries = [flip(x, 1) for x in (keys, values, queries)]
        mine = pl.pallas_call(
            functools.partial(pick_kernel, where),
            out_shape=shape((4, 2, BLK, width), BF16),
            in_specs=[HBM] * 2,
            out_specs=VMEM,
            scratch_shapes=[dma],
            compiler_params=params(53),
            cost_estimate=cost(1, 1),
            name="pick",
        )(keys, values)
        sent = pl.pallas_call(
            functools.partial(pair_kernel, where),
            out_shape=[shape((2, 2, BLK, width), BF16)] * 4,
            in_specs=[VMEM] * 3,
            out_specs=[VMEM] * 4,
            compiler_params=params(4),
            cost_estimate=cost(3*10**9, 1),
            name="pair",
        )(mine, *theirs)
        kv = [sent[0]] + [flip(sent[j], 2 * j) for j in range(1, 4)]
        layout = [(j, 0, 2, lambda m, j=j: (m ^ (2 * j)) // 2 * 2) for j in range(4)]
        q_layout = layout
        first = onward(kv[0], 1)
        *q, rates = pl.pallas_call(
            functools.partial(pair_queries_kernel, where),
            out_shape=[shape((2, BLK, width), BF16)] * 4 + [shape((heads, 8, BLK), F32)],
            in_specs=[SMEM] + [VMEM] * 2 + [ANY],
            out_specs=[VMEM] * 5,
            compiler_params=params(4),
            cost_estimate=cost(1, 1),
            name="pair_queries",
        )(step_rate, queries, their_queries, kv[0])
        second = onward(hold(kv[1:2], q[1]), 1)
        far = [first, second, onward(kv[2], 1)]
        far_layout = layout
        earlier = [second, first]
        ready = []
        q = [q[0]] + [flip(q[j], 2 * j) for j in range(1, 4)]
    else:
        earlier = []
        ready = []
        rates = lax.dynamic_slice_in_dim(step_rate, member * heads, heads)
        rates = jnp.broadcast_to(rates[:, None, None], (heads, 8, BLK))
        def by_heads(parts):
            parts = parts.reshape(-1, tokens // BLK, BLK, group_size, width)
            parts = parts.transpose(3, 1, 0, 2, 4)
            if group_size > 1:
                parts = lax.all_to_all(parts, axis, 0, 0, axis_index_groups=members, tiled=True)
            return parts.reshape(blocks, -1, BLK, width)

        kv = [by_heads(jnp.stack([keys, values]))]
        q = [by_heads(queries)[:, 0]]
        far = [onward(kv[0], distance) for distance in range(WIN // span, 0, -1)]
        layout = q_layout = [(0, 0, blocks, lambda m: 0)]
        ready = []
        far_layout = [(c, 0, blocks, lambda m, c=c: c * blocks) for c in range(len(far))]

    total, before, inject = pl.pallas_call(
        functools.partial(memory_kernel, layout, where),
        out_shape=[
            shape((heads, BLK, 2 * BLK), BF16),
            shape((blocks, heads, BLK, 2 * BLK), BF16),
            shape((blocks, heads, BLK, 2 * BLK), BF16),
        ],
        in_specs=[VMEM] * (1 + len(kv)) + [ANY] * len(earlier),
        out_specs=[VMEM] * 3,
        scratch_shapes=[pltpu.VMEM((blocks, 2, BLK, width), BF16)],
        compiler_params=params(12),
        cost_estimate=cost(50 * 10**8, 1),
        name="memory_updates",
    )(rates, *kv, *earlier)

    near, logs, lin, off = pl.pallas_call(
        functools.partial(local_kernel, layout, q_layout, where),
        out_shape=[
            shape((heads, blocks, BLK, BLK), F32),
            state_shape,
            shape((heads, blocks, BLK, BLK), BF16),
            shape((heads, blocks, BLK, BLK), F32),
        ],
        in_specs=[VMEM] * (len(kv) + len(q) + 2) + [ANY] * len(ready),
        out_specs=[VMEM] * 4,
        scratch_shapes=[
            pltpu.VMEM((blocks, BLK, width), BF16),
            pltpu.VMEM((blocks, 2, BLK, width), BF16),
        ],
        compiler_params=params(12),
        cost_estimate=cost(40 * 10**8, 1),
        name="attend_own",
    )(*kv, *q, before, inject, *ready)
    if direct:
        held = flip(total, group_size)
        far.append(onward(hold(kv[3:], total), 1))
        own, after = pl.pallas_call(
            functools.partial(after_kernel, where),
            out_shape=[state_shape, shape((heads, BLK, BLK), BF16)],
            in_specs=[VMEM] * 3 + [ANY],
            out_specs=[VMEM, VMEM],
            compiler_params=params(8),
            cost_estimate=cost(1, 1),
            name="state_after",
        )(held, total, memory_init, far[2])
        moved = flip(after, 2 * group_size)
    else:
        updates = lax.all_gather(
            total, axis, axis_index_groups=[list(x) for x in zip(*members)]
        )
        own = pl.pallas_call(
            functools.partial(chain_kernel, where),
            out_shape=state_shape,
            in_specs=[VMEM, HBM],
            out_specs=VMEM,
            scratch_shapes=[dma],
            compiler_params=params(32),
            name="state_chain",
        )(updates, memory_init)
        moved, held = own.astype(BF16), total

    attended = pl.pallas_call(
        functools.partial(far_kernel, far_layout, q_layout, where),
        out_shape=shape((heads, blocks, BLK, BLK), F32),
        in_specs=[VMEM] * (2 + len(far) + len(q)),
        out_specs=VMEM,
        scratch_shapes=[
            pltpu.VMEM((blocks, BLK, width), BF16),
            pltpu.VMEM((reach, 2, BLK, width), BF16),
        ],
        compiler_params=params(12),
        cost_estimate=cost(4 * 10**9, 1),
        name="attend_far",
    )(near, logs, *far, *q)
    gated = pl.pallas_call(
        functools.partial(gate_kernel, where),
        out_shape=[shape((tokens, width), BF16)] * group_size,
        in_specs=[VMEM] * 6,
        out_specs=[VMEM] * group_size,
        compiler_params=params(8),
        cost_estimate=cost(10**9, 1),
        name="gate",
    )(attended, lin, off, own, moved, held)
    gated = [gated[0]] + [flip(gated[s], s) for s in range(1, group_size)]
    features = out_weight.shape[1]
    split_out = lax.axis_size("tp") > 1
    part = []
    early = list(range(7 if group_size == 8 else 0))
    if early:
        part = [
            pl.pallas_call(
                functools.partial(partial_kernel, early, where),
                out_shape=shape((tokens, features), F32),
                in_specs=[VMEM] * (1 + len(early)),
                out_specs=VMEM,
                compiler_params=params(8),
                cost_estimate=cost(10**9, 1),
                name="project_early",
            )(out_weight, *[gated[s] for s in early])
        ]
    late = list(range(len(early), group_size))
    kind = F32 if split_out else BF16
    projected = pl.pallas_call(
        functools.partial(project_kernel, late, where),
        out_shape=shape((tokens, features), kind),
        in_specs=[VMEM] * (1 + len(late) + len(part)),
        out_specs=HBM,
        scratch_shapes=[pltpu.VMEM((tokens, features), kind), dma],
        compiler_params=params(8),
        cost_estimate=cost(10**9, 1),
        name="project",
    )(out_weight, *[gated[s] for s in late], *part)
    if split_out:
        projected = lax.psum_scatter(projected, "tp", scatter_dimension=1, tiled=True)
    return projected.astype(BF16)


def solution(mesh):
    return jax.shard_map(
        shards,
        mesh=mesh,
        in_specs=(
            P("seq", "tp"),
            P("seq", "tp"),
            P("seq", "tp"),
            P("tp"),
            P("tp", None, None),
            P("tp", None),
        ),
        out_specs=P("seq", "tp"),
        check_vma=False,
    )
```
